1024 devices in a mesh: hs: 32 (over z_hi, y, x), tok: 32 (over z_lo, core).
Axes of the slice: x: 4, y: 4, z: 32 (z_hi: 2, z_lo: 16; z = z_hi * 16 + z_lo), core: 2. Of those that a mesh axis runs over, the one named last changes fastest.
Arguments:
- queries: bfloat16 [2, 32, 4096, 384], P(None, 'hs', 'tok'), may hold values from -8 to 8
- out_grads: bfloat16 [2, 32, 4096, 384], P(None, 'hs', 'tok'), may hold values from -6 to 6
- kv_cache: bfloat16 [32, 4096, 256], P('hs', 'tok'), may hold values from -8 to 8
- features: bfloat16 [32, 4096, 384], P('hs', 'tok'), may hold values from -6 to 6
- doc_lens: int32 [4, 4], replicated, may hold values from 1 to 2048, as said below
Outputs:
- query_grads: bfloat16 [2, 32, 4096, 384], P(None, 'hs', 'tok')
- cache_grads: bfloat16 [32, 4096, 256], P('hs', 'tok')
- kv_weight_grads: float32 [3072, 2048], P('tok', 'hs')
The draws below stay inside these ranges and needn't reach their ends.
Inputs may be any that keep to these rules, and one draw needn't show every extreme that they name: `doc_lens`: each row sums to 4096; in every row the longest document has exactly 2048 tokens, is the second or third document, and starts 128 // 4 to 96 positions after the start of a token shard.
All inputs are finite; a program needn't handle non-finite values.
Results may differ from the reference program's by a relative error of at most 0.024.
Values may be sent and summed in bfloat16 or wider, within the bound.
A program may use at most 32 MiB of HBM per device.

```python
import jax
import jax.numpy as jnp
from jax import lax

D = 3072
HD = 128
LAYERS = 2
T_DEV = 128
HEAD_RANKS = 8
SEQS = 4
KV_DEV = 1
QH_DEV = 3
FEAT_DEV = 384
LEN = 4096
GROUPS = 32
N_TOK = 32


START_KEY = 2.0


START_PULL = 3.0


def start_pattern(key):
    coin_flips = jax.random.bernoulli(jax.random.fold_in(key, 202), 0.5, (HD,))
    return jnp.where(coin_flips, 1.0, -1.0).astype(jnp.float32)


def doc_layout(key):
    key = jax.random.fold_in(key, 303)
    slot_key, block_key, offset_key, cut_key = jax.random.split(key, 4)
    half_len = LEN // 2
    slot = jax.random.randint(slot_key, (SEQS,), 1, 3)
    blocks = jax.random.randint(block_key, (SEQS,), 0, half_len // T_DEV)
    offsets = jax.random.randint(offset_key, (SEQS,), T_DEV // 4, 3 * T_DEV // 4 + 1)
    start = (blocks * T_DEV + offsets).astype(jnp.int32)
    region = jnp.where(slot == 1, half_len - start, start).astype(jnp.int32)
    cut = jax.random.randint(cut_key, (SEQS,), 1, region).astype(jnp.int32)
    half_col = jnp.full((SEQS,), half_len, jnp.int32)
    first_form = jnp.stack([start, half_col, cut, region - cut], axis=1)
    second_form = jnp.stack([cut, region - cut, half_col, half_len - start], axis=1)
    return jnp.where((slot == 1)[:, None], first_form, second_form).astype(jnp.int32)


def draw_doc_lens(key, part):
    return doc_layout(key)


def draw_queries(key, part):
    start_row = start_pattern(key)
    key = jax.random.fold_in(key, 3)
    full_shape = (LAYERS, GROUPS, LEN, QH_DEV, HD)
    pull = START_PULL * HD ** (-0.5) * start_row
    values = jnp.clip(jax.random.normal(key, full_shape, jnp.float32), -6.0, 6.0) + pull
    return values.reshape(LAYERS, GROUPS, LEN, QH_DEV * HD).astype(jnp.bfloat16)


def draw_kv_cache(key, part):
    start_row = start_pattern(key)
    lengths = doc_layout(key)
    key = jax.random.fold_in(key, 5)
    full_shape = (GROUPS, LEN, KV_DEV, 2, HD)
    starts = jnp.cumsum(lengths, axis=1) - lengths
    positions = jnp.arange(LEN, dtype=jnp.int32)
    is_start = jnp.any(positions[None, None, :] == starts[:, :, None], axis=1)
    group_start = is_start[jnp.arange(GROUPS, dtype=jnp.int32) % SEQS]
    start_key = START_KEY * start_row
    values = jnp.clip(jax.random.normal(key, full_shape, jnp.float32), -6.0, 6.0)
    values = values.at[:, :, :, 0].set(jnp.where(group_start[:, :, None, None], start_key, values[:, :, :, 0]))
    return values.reshape(GROUPS, LEN, 2 * KV_DEV * HD).astype(jnp.bfloat16)


def levels(rng, extent, cuts, low, top_value):
    level, own = 1.0, jax.random.fold_in(rng, 6)
    for dim, parts in cuts:
        steps = jnp.exp(jax.random.uniform(jax.random.fold_in(own, dim), (parts,), jnp.float32, low / len(cuts), top_value / len(cuts)))
        level = level * jnp.repeat(steps, extent[dim] // parts).reshape([-1 if axis == dim else 1 for axis in range(len(extent))])
    return level


def gaussian(stream_key, shape, width, bound, cuts=(), kind=jnp.bfloat16):
    array = width * jax.random.normal(stream_key, shape, jnp.float32)
    if cuts:
        array = array * levels(stream_key, shape, cuts, -0.22, 0.18)
    return jnp.clip(array, -bound, bound).astype(kind)


def setup_inputs(seed: int = 0) -> dict:
    seeds = jax.random.split(jax.random.key(seed), 6)
    queries = draw_queries(jax.random.fold_in(seeds[5], 71), 0)
    out_grads = gaussian(seeds[1], (LAYERS, GROUPS, LEN, QH_DEV * HD), 1.0, 6.0, ((1, 32), (2, 32)))
    kv_cache = draw_kv_cache(jax.random.fold_in(seeds[5], 71), 0)
    features = gaussian(seeds[3], (GROUPS, LEN, FEAT_DEV), 1.0, 6.0, ((0, 32), (1, 32)))
    doc_lens = draw_doc_lens(jax.random.fold_in(seeds[5], 71), 0)
    return {"queries": queries, "out_grads": out_grads, "kv_cache": kv_cache, "features": features, "doc_lens": doc_lens}


NEG_FILL = -1.0e30


def doc_index(lengths, positions):
    doc_ends = jnp.cumsum(lengths).astype(jnp.int32)
    return jnp.sum((positions[:, None] >= doc_ends[None, :]).astype(jnp.int32), axis=1)


def round_trip(values):
    rounded = lax.optimization_barrier(values.astype(jnp.bfloat16))
    return rounded.astype(jnp.float32)


def group_grads(query_all, upstream_all, cache, lengths):
    group_size = QH_DEV // KV_DEV
    score_scale = HD ** -0.5
    cache_wide = cache.astype(jnp.float32).reshape(LEN, KV_DEV, 2, HD)
    keys_all = cache_wide[:, :, 0]
    values_all = cache_wide[:, :, 1]
    key_pos = jnp.arange(LEN, dtype=jnp.int32)
    key_doc = doc_index(lengths, key_pos)

    def shard_step(accumulated, shard_number):
        first_row = (shard_number * T_DEV).astype(jnp.int32)
        query_rows = lax.dynamic_slice_in_dim(query_all, first_row, T_DEV, 1).astype(jnp.float32)
        query_rows = query_rows.reshape(LAYERS, T_DEV, KV_DEV, group_size, HD)
        upstream = lax.dynamic_slice_in_dim(upstream_all, first_row, T_DEV, 1).astype(jnp.float32)
        upstream = upstream.reshape(LAYERS, T_DEV, KV_DEV, group_size, HD)
        query_pos = first_row + jnp.arange(T_DEV, dtype=jnp.int32)
        query_doc = doc_index(lengths, query_pos)
        allowed = (key_pos[None, :] <= query_pos[:, None]) & (key_doc[None, :] == query_doc[:, None])
        scores = jnp.einsum("ltgrd,kgd->lgrtk", query_rows, keys_all) * score_scale
        row_top = jnp.max(jnp.where(allowed, scores, NEG_FILL), axis=-1, keepdims=True)
        exp_terms = jnp.where(allowed, jnp.exp(scores - row_top), 0.0)
        weights = exp_terms / jnp.sum(exp_terms, axis=-1, keepdims=True)
        dweights = jnp.einsum("ltgrd,kgd->lgrtk", upstream, values_all)
        row_delta = jnp.sum(weights * dweights, axis=-1, keepdims=True)
        dscores = round_trip(weights * (dweights - row_delta))
        weights_b = round_trip(weights)
        dquery = score_scale * jnp.einsum("lgrtk,kgd->ltgrd", dscores, keys_all)
        dquery = dquery.reshape(LAYERS, T_DEV, QH_DEV * HD).astype(jnp.bfloat16)
        key_grads = score_scale * jnp.einsum("lgrtk,ltgrd->kgd", dscores, query_rows)
        dvalues = jnp.einsum("lgrtk,ltgrd->kgd", weights_b, upstream)
        shard_term = jnp.stack([key_grads, dvalues], axis=2).reshape(LEN, 2 * KV_DEV * HD)
        return accumulated + round_trip(shard_term), dquery

    accumulated, dquery = lax.scan(shard_step, jnp.zeros((LEN, 2 * KV_DEV * HD), jnp.float32),
                                   jnp.arange(N_TOK, dtype=jnp.int32))
    dquery = jnp.transpose(dquery, (1, 0, 2, 3)).reshape(LAYERS, LEN, QH_DEV * HD)
    return dquery, accumulated.astype(jnp.bfloat16)


def reference(queries, out_grads, kv_cache, features, doc_lens):
    def one_group(group_number):
        sequence = group_number % SEQS
        lengths = lax.dynamic_index_in_dim(doc_lens, sequence, 0, keepdims=False)
        query_all = lax.dynamic_index_in_dim(queries, group_number, 1, keepdims=False)
        upstream_all = lax.dynamic_index_in_dim(out_grads, group_number, 1, keepdims=False)
        cache = lax.dynamic_index_in_dim(kv_cache, group_number, 0, keepdims=False)
        return group_grads(query_all, upstream_all, cache, lengths)

    dquery, cache_grads = lax.map(one_group, jnp.arange(GROUPS, dtype=jnp.int32))
    query_grads = jnp.transpose(dquery, (1, 0, 2, 3))
    full_features = [jnp.concatenate([features[head_rank * SEQS + sequence] for head_rank in range(HEAD_RANKS)], axis=1)
                     for sequence in range(SEQS)]
    columns = []
    for head_rank in range(HEAD_RANKS):
        column_sum = jnp.zeros((D, 2 * KV_DEV * HD), jnp.float32)
        for sequence in range(SEQS):
            column_sum = column_sum + jnp.dot(full_features[sequence].T, cache_grads[head_rank * SEQS + sequence],
                                              preferred_element_type=jnp.float32)
        columns.append(column_sum)
    return query_grads, cache_grads, jnp.concatenate(columns, axis=1)
```

```python
import functools

import jax
import jax.numpy as jnp
from jax import lax
from jax.experimental import pallas as pl
from jax.experimental.pallas import tpu as pltpu
from jax.sharding import PartitionSpec as P

HD = 128
KVH = 8
NEG_FILL = -1e30
PIECES = 2
LOG2E = 1.4426950408889634
CONTRACT_LAST = (((1,), (1,)), ((), ()))
CONTRACT_FIRST = (((0,), (0,)), ((), ()))


def remote(src, dst, send_sem, recv_sem, tok):
    return pltpu.make_async_remote_copy(
        src_ref=src,
        dst_ref=dst,
        send_sem=send_sem,
        recv_sem=recv_sem,
        device_id={"tok": tok},
        device_id_type=pl.DeviceIdType.MESH,
    )


def attention_kernel(
    n_tok,
    doc_lens,
    queries,
    upstream,
    cache,
    query_grads,
    cache_grads,
    qs,
    us,
    window,
    exps,
    dws,
    tops,
    stats,
    dq_acc,
    terms,
    own_terms,
    sib_out,
    sib_in,
    run_out,
    run_in,
    up_send,
    up_recv,
    side_send,
    side_recv,
    back_side_send,
    back_side_recv,
    down_send,
    down_recv,
):
    layers, rows, columns = queries.shape
    heads = columns // HD
    n_rows = layers * heads * rows
    chips = n_tok // 2
    reach = n_tok // 4
    piece = rows // PIECES
    pair = 2 * rows
    n_pairs = n_rows // pair
    scale = HD ** (-0.5)

    tok = lax.axis_index("tok")
    hs = lax.axis_index("hs")
    chip = tok // 2
    core = tok % 2
    sibling = tok + 1 - 2 * core
    above = lax.rem(tok + 2, n_tok)
    below = lax.rem(tok + n_tok - 2, n_tok)
    not_last = chip < chips - 1
    mine = core * rows
    theirs = (1 - core) * rows

    barrier = pltpu.get_barrier_semaphore()
    for other in (sibling, above, below):
        pl.semaphore_signal(
            barrier, inc=1, device_id={"tok": other}, device_id_type=pl.DeviceIdType.MESH
        )
    pl.semaphore_wait(barrier, 3)

    def span(first, i):
        return pl.ds(pl.multiple_of(first + i * piece, piece), piece)

    def up_copy(d, i, from_cache=False):
        src = cache.at[pl.ds(i * piece, piece)] if from_cache else window.at[d - 1, span(mine, i)]
        return remote(src, window.at[d, span(mine, i)], up_send.at[d, i], up_recv.at[d, i], above)

    def side_copy(d, i, from_cache=False):
        src = cache.at[pl.ds(i * piece, piece)] if from_cache else window.at[d, span(mine, i)]
        return remote(
            src, window.at[d, span(mine, i)], side_send.at[d, i], side_recv.at[d, i], sibling
        )

    def side_arrival(d, i):
        dst = window.at[d, span(theirs, i)]
        return remote(dst, dst, side_send.at[d, i], side_recv.at[d, i], sibling)

    for i in range(PIECES):

        @pl.when(not_last)
        def _():
            up_copy(1, i, True).start()

        side_copy(0, i, True).start()

    window[0, pl.ds(pl.multiple_of(mine, rows), rows)] = cache[...]
    for layer in range(layers):
        for head in range(heads):
            at = (layer * heads + head) * rows
            qs[at : at + rows] = queries[layer, :, head * HD : (head + 1) * HD]
            us[at : at + rows] = upstream[layer, :, head * HD : (head + 1) * HD]

    row_top = stats.at[0:1]
    row_total = stats.at[1:2]
    row_weighted = stats.at[2:3]
    row_top[...] = jnp.full((1, n_rows), NEG_FILL, jnp.float32)
    row_total[...] = jnp.zeros((1, n_rows), jnp.float32)
    row_weighted[...] = jnp.zeros((1, n_rows), jnp.float32)

    seq = hs % doc_lens.shape[0]
    position = tok * rows + lax.rem(lax.broadcasted_iota(jnp.int32, (1, pair), 1), rows)
    start = jnp.zeros((1, pair), jnp.int32)
    end = jnp.int32(0)
    for k in range(doc_lens.shape[1] - 1):
        end = end + doc_lens[seq, k]
        start = jnp.where(position >= end, end, start)

    for i in range(PIECES):
        side_arrival(0, i).wait_recv()

    def stats_part(d, n):
        at = pl.ds(n * pair, pair)
        key_rows = window[d, :, 0:HD]
        value_rows = window[d, :, HD : 2 * HD]
        scores = lax.dot_general(
            key_rows, qs[at], CONTRACT_LAST, preferred_element_type=jnp.float32
        )
        dweights = lax.dot_general(
            value_rows, us[at], CONTRACT_LAST, preferred_element_type=jnp.float32
        )
        key_pos = (chip - d) * pair + lax.broadcasted_iota(jnp.int32, (pair, pair), 0)
        allowed = (key_pos <= position) & (key_pos >= start)
        scores = jnp.where(allowed, scores * (scale * LOG2E), NEG_FILL)
        top_old = row_top[:, at]
        top = jnp.maximum(top_old, jnp.max(scores, axis=0, keepdims=True))
        exp_terms = jnp.exp2(scores - top)
        factor = jnp.exp2(top_old - top)
        row_top[:, at] = top
        row_total[:, at] = row_total[:, at] * factor + jnp.sum(exp_terms, axis=0, keepdims=True)
        row_weighted[:, at] = row_weighted[:, at] * factor + jnp.sum(
            exp_terms * dweights, axis=0, keepdims=True
        )
        exps[d, :, at] = exp_terms
        dws[d, :, at] = dweights
        tops[d, :, at] = top

    @pl.loop(0, reach + 1)
    def _(d):
        more = (d < reach) & (chip > d)
        for n in range(n_pairs):

            @pl.when(chip >= d)
            def _():
                stats_part(d, n)

            if n < PIECES:

                @pl.when(more)
                def _():
                    up_copy(d + 1, n).wait_recv()
                    side_copy(d + 1, n).start()

                @pl.when(more & not_last & (d + 1 < reach))
                def _():
                    up_copy(d + 2, n).start()

        @pl.when(more)
        def _():
            for i in range(PIECES):
                side_arrival(d + 1, i).wait_recv()

    inverse = 1.0 / row_total[...]
    row_delta = stats.at[3:4]
    row_delta[...] = row_weighted[...] * inverse
    row_total[...] = inverse
    dq_acc[...] = jnp.zeros_like(dq_acc)
    run_in[reach] = jnp.zeros((rows, 2 * HD), jnp.bfloat16)

    @pl.when(chip == chips - 1)
    def _():
        for d in range(reach):
            run_in[d] = jnp.zeros((rows, 2 * HD), jnp.bfloat16)

    def grads_part(d, n):
        at = pl.ds(n * pair, pair)
        factor = jnp.exp2(tops[d, :, at] - row_top[:, at]) * row_total[:, at]
        weights = exps[d, :, at] * factor
        dscores = (weights * (dws[d, :, at] - row_delta[:, at])).astype(jnp.bfloat16)
        weights = weights.astype(jnp.bfloat16)
        key_rows = window[d, :, 0:HD]
        key_grads = jnp.dot(dscores, qs[at], preferred_element_type=jnp.float32)
        dvalues = jnp.dot(weights, us[at], preferred_element_type=jnp.float32)
        if n == 0:
            terms[:, 0:HD] = key_grads
            terms[:, HD : 2 * HD] = dvalues
        else:
            terms[:, 0:HD] += key_grads
            terms[:, HD : 2 * HD] += dvalues
        dq_acc[:, at] += lax.dot_general(
            key_rows, dscores, CONTRACT_FIRST, preferred_element_type=jnp.float32
        )

    def back_side_copy(d, i):
        at = pl.ds(i * piece, piece)
        return remote(
            sib_out.at[d, at],
            sib_in.at[d, at],
            back_side_send.at[d, i],
            back_side_recv.at[d, i],
            sibling,
        )

    def down_copy(d, i):
        at = pl.ds(i * piece, piece)
        return remote(
            run_out.at[d, at], run_in.at[d - 1, at], down_send.at[d, i], down_recv.at[d - 1, i], below
        )

    def down_arrival(d, i):
        at = pl.ds(i * piece, piece)
        return remote(
            run_out.at[d, at], run_in.at[d, at], down_send.at[d, i], down_recv.at[d, i], below
        )

    def chain_part(d, i):
        back_side_copy(d, i).wait_recv()

        @pl.when(not_last & (d < reach))
        def _():
            down_arrival(d, i).wait_recv()

        at = pl.ds(i * piece, piece)
        return (
            own_terms[d, at]
            + sib_in[d, at].astype(jnp.float32)
            + run_in[d, at].astype(jnp.float32)
        ).astype(jnp.bfloat16)

    def chain_send(d, i):
        run_out[d, pl.ds(i * piece, piece)] = chain_part(d, i)
        down_copy(d, i).start()

    @pl.loop(0, reach + 1)
    def _(step):
        d = reach - step
        for n in range(n_pairs):

            @pl.when(chip >= d)
            def _():
                grads_part(d, n)

            if n < PIECES:

                @pl.when((step > 0) & (chip >= d + 1))
                def _():
                    chain_send(d + 1, n)

        @pl.when(chip >= d)
        def _():
            sent = terms[pl.ds(pl.multiple_of(theirs, rows), rows)]
            sib_out[d, :, 0:HD] = (sent[:, 0:HD] * scale).astype(jnp.bfloat16)
            sib_out[d, :, HD : 2 * HD] = sent[:, HD : 2 * HD].astype(jnp.bfloat16)
            for i in range(PIECES):
                back_side_copy(d, i).start()
            kept = terms[pl.ds(pl.multiple_of(mine, rows), rows)]
            own_terms[d, :, 0:HD] = kept[:, 0:HD] * scale
            own_terms[d, :, HD : 2 * HD] = kept[:, HD : 2 * HD]

    for layer in range(layers):
        for head in range(heads):
            at = (layer * heads + head) * rows
            block = jnp.transpose(dq_acc[:, at : at + rows]) * scale
            query_grads[layer, :, head * HD : (head + 1) * HD] = block.astype(jnp.bfloat16)
    for i in range(PIECES):
        cache_grads[pl.ds(i * piece, piece)] = chain_part(0, i)

    @pl.loop(0, reach + 1)
    def _(d):
        for i in range(PIECES):

            @pl.when(chip >= d)
            def _():
                side_copy(d, i).wait_send()
                back_side_copy(d, i).wait_send()

            @pl.when((chip >= d) & (d > 0))
            def _():
                down_copy(d, i).wait_send()

            @pl.when(not_last & (chip + 1 >= d) & (d > 0))
            def _():
                up_copy(d, i).wait_send()


def attention(queries, out_grads, cache, doc_lens):
    layers, rows, columns = queries.shape
    n_tok = lax.axis_size("tok")
    slots = n_tok // 4 + 1
    n_rows = layers * columns // HD * rows
    pair = 2 * rows
    vmem = pl.BlockSpec(memory_space=pltpu.VMEM)
    sems = pltpu.SemaphoreType.DMA((slots, PIECES))
    block = (slots, rows, 2 * HD)
    return pl.pallas_call(
        functools.partial(attention_kernel, n_tok),
        out_shape=(
            jax.ShapeDtypeStruct(queries.shape, jnp.bfloat16),
            jax.ShapeDtypeStruct(cache.shape, jnp.bfloat16),
        ),
        in_specs=[pl.BlockSpec(memory_space=pltpu.SMEM), vmem, vmem, vmem],
        out_specs=(vmem, vmem),
        scratch_shapes=[
            pltpu.VMEM((n_rows, HD), jnp.bfloat16),
            pltpu.VMEM((n_rows, HD), jnp.bfloat16),
            pltpu.VMEM((slots, pair, 2 * HD), jnp.bfloat16),
            pltpu.VMEM((slots, pair, n_rows), jnp.float32),
            pltpu.VMEM((slots, pair, n_rows), jnp.float32),
            pltpu.VMEM((slots, 1, n_rows), jnp.float32),
            pltpu.VMEM((8, n_rows), jnp.float32),
            pltpu.VMEM((HD, n_rows), jnp.float32),
            pltpu.VMEM((pair, 2 * HD), jnp.float32),
            pltpu.VMEM(block, jnp.float32),
            pltpu.VMEM(block, jnp.bfloat16),
            pltpu.VMEM(block, jnp.bfloat16),
            pltpu.VMEM(block, jnp.bfloat16),
            pltpu.VMEM(block, jnp.bfloat16),
        ]
        + [sems] * 8,
        compiler_params=pltpu.CompilerParams(
            collective_id=0, has_side_effects=True, vmem_limit_bytes=40 * 2**20
        ),
        name="attention",
    )(doc_lens, queries, out_grads, cache)


def from_partner(value, axis, bit):
    mask = 2**bit
    pairs = [(source, source ^ mask) for source in range(lax.axis_size(axis))]
    return lax.ppermute(value, axis, pairs)


def halve_block(total_sum, upper_bit, which_dim):
    half_width = total_sum.shape[which_dim] // 2
    lower_part = lax.slice_in_dim(total_sum, 0, half_width, axis=which_dim)
    upper_part = lax.slice_in_dim(total_sum, half_width, 2 * half_width, axis=which_dim)
    kept_part = jnp.where(upper_bit == 1, upper_part, lower_part)
    sent_part = jnp.where(upper_bit == 1, lower_part, upper_part)
    return (kept_part, sent_part)


def shards(queries, out_grads, kv_cache, features, doc_lens):
    hs_count = lax.axis_size("hs")
    tok_count = lax.axis_size("tok")
    rank_count = min(KVH, hs_count)
    seq_count = hs_count // rank_count
    hs_place = lax.axis_index("hs")
    query_grads, summed = attention(queries[:, 0], out_grads[:, 0], kv_cache[0], doc_lens)
    full_rows = features[0]
    seq_bits = seq_count.bit_length() - 1
    hs_bits = hs_count.bit_length() - 1
    tok_bits = tok_count.bit_length() - 1
    for bit_number in range(seq_bits, hs_bits):
        partner = from_partner(full_rows, "hs", bit_number)
        upper_bit = hs_place >> bit_number & 1
        full_rows = jnp.where(
            upper_bit == 1,
            jnp.concatenate([partner, full_rows], axis=1),
            jnp.concatenate([full_rows, partner], axis=1),
        )
    partial_grads = jnp.einsum("tf,tc->fc", full_rows, summed, preferred_element_type=jnp.float32)
    joined_place = lax.axis_index(("hs", "tok"))
    halvings = [(tok_bits + bit_number, 1) for bit_number in reversed(range(seq_bits))]
    halvings = halvings + [(bit_number, 0) for bit_number in reversed(range(tok_bits))]
    weight_total = partial_grads
    for bit_number, which_dim in halvings:
        upper_bit = joined_place >> bit_number & 1
        kept_part, sent_part = halve_block(weight_total, upper_bit, which_dim)
        weight_total = kept_part + from_partner(
            sent_part.astype(jnp.bfloat16), ("hs", "tok"), bit_number
        ).astype(sent_part.dtype)
    return (query_grads[:, None], summed[None], weight_total)


def solution(mesh):
    placed = (
        P(None, "hs", "tok", None),
        P(None, "hs", "tok", None),
        P("hs", "tok", None),
        P("hs", "tok", None),
        P(),
    )
    return jax.shard_map(
        shards,
        mesh=mesh,
        in_specs=placed,
        out_specs=(P(None, "hs", "tok", None), P("hs", "tok", None), P("tok", "hs")),
        check_vma=False,
    )
```

```python
import functools

import jax
import jax.numpy as jnp
from jax import lax
from jax.experimental import pallas as pl
from jax.experimental.pallas import tpu as pltpu
from jax.sharding import PartitionSpec as P

HD = 128
SEQS = 4
RANKS_Y = 4
GROUP = 4
NEG_FILL = -1e30
PIECES = 2
CROSS_AT = "mid"
LOG2E = 1.4426950408889634
MESH = pl.DeviceIdType.MESH
CONTRACT_LAST = (((1,), (1,)), ((), ()))
CONTRACT_FIRST = (((0,), (0,)), ((), ()))


def remote(src, dst, send_sem, recv_sem, device):
    return pltpu.make_async_remote_copy(
        src_ref=src,
        dst_ref=dst,
        send_sem=send_sem,
        recv_sem=recv_sem,
        device_id=device,
        device_id_type=MESH,
    )


def kernel(
    n_tok,
    doc_lens,
    queries,
    upstream,
    cache,
    features,
    query_grads,
    cache_grads,
    weight_grads,
    qs,
    us,
    window,
    exps,
    dws,
    tops,
    stats,
    dq_acc,
    terms,
    own_terms,
    sib_out,
    sib_in,
    run_out,
    run_in,
    feat_own,
    feat_cross,
    feat_all,
    grads_out,
    grads_in,
    parts,
    core_in,
    near_out,
    near_in,
    far_out,
    far_in,
    last_out,
    last_in,
    up_send,
    up_recv,
    side_send,
    side_recv,
    back_send,
    back_recv,
    down_send,
    down_recv,
    own_send,
    cross_send,
    feat_recv,
    half_send,
    half_recv,
    grads_send,
    grads_recv,
    core_send,
    core_recv,
    near_send,
    near_recv,
    far_send,
    far_recv,
    last_send,
    last_recv,
):
    layers, rows, columns = queries.shape
    heads = columns // HD
    n_rows = layers * heads * rows
    chips = n_tok // 2
    reach = n_tok // 4
    piece = rows // PIECES
    pair = 2 * rows
    n_pairs = n_rows // pair
    scale = HD ** (-0.5)

    tok = lax.axis_index("tok")
    hs = lax.axis_index("hs")
    chip = tok // 2
    core = tok % 2
    sibling = tok + 1 - 2 * core
    mine = core * rows
    theirs = (1 - core) * rows
    x = hs % SEQS
    y = (hs // SEQS) % RANKS_Y
    plane = SEQS * RANKS_Y
    half = hs // plane
    place = hs % plane
    rank = half * RANKS_Y + y
    other_half = (1 - half) * plane + place
    other_rank = (1 - half) * RANKS_Y + y
    beside = hs + 1 - 2 * (x % 2)
    spot = chip % GROUP
    group = chip // GROUP

    def near_tok(k):
        return (group * GROUP + (spot + k) % GROUP) * 2 + core

    def far_tok(k):
        return (((group + k) % GROUP) * GROUP + spot) * 2 + core

    def plane_hs(k):
        return half * plane + (place + k) % plane

    barrier = pltpu.get_barrier_semaphore()
    met = [{"tok": sibling}]
    met += [{"tok": (tok + k) % n_tok} for k in (2, n_tok - 2, 6, n_tok - 6)]
    met += [{"tok": near_tok(k)} for k in range(1, GROUP)]
    met += [{"tok": far_tok(k)} for k in range(1, GROUP)]
    met += [{"hs": plane_hs(k)} for k in range(1, plane)]
    met += [{"hs": other_half}, {"hs": beside, "tok": sibling}]
    for device in met:
        pl.semaphore_signal(barrier, inc=1, device_id=device, device_id_type=MESH)

    for layer in range(layers):
        for head in range(heads):
            at = (layer * heads + head) * rows
            qs[at : at + rows] = queries[layer, :, head * HD : (head + 1) * HD]
            us[at : at + rows] = upstream[layer, :, head * HD : (head + 1) * HD]
    window[0, pl.ds(pl.multiple_of(mine, rows), rows)] = cache[...]

    row_block = features.shape[1] // 4
    for n in range(features.shape[1] // HD):
        turned = jnp.transpose(features[:, n * HD : (n + 1) * HD].astype(jnp.float32)).astype(
            jnp.bfloat16
        )
        first = n * HD
        while first < (n + 1) * HD:
            block = first // row_block
            last = min((block + 1) * row_block, (n + 1) * HD)
            to = (block // 2) * row_block + first - block * row_block
            feat_own[block % 2, to : to + last - first] = turned[
                first - n * HD : last - n * HD
            ]
            first = last

    row_top = stats.at[0:1]
    row_total = stats.at[1:2]
    row_weighted = stats.at[2:3]
    row_top[...] = jnp.full((1, n_rows), NEG_FILL, jnp.float32)
    row_total[...] = jnp.zeros((1, n_rows), jnp.float32)
    row_weighted[...] = jnp.zeros((1, n_rows), jnp.float32)
    dq_acc[...] = jnp.zeros_like(dq_acc)

    seq = x
    position = tok * rows + lax.rem(lax.broadcasted_iota(jnp.int32, (1, pair), 1), rows)
    start = jnp.zeros((1, pair), jnp.int32)
    end = jnp.int32(0)
    for k in range(doc_lens.shape[1] - 1):
        end = end + doc_lens[seq, k]
        start = jnp.where(position >= end, end, start)

    pl.semaphore_wait(barrier, len(met))

    def span(first, i):
        return pl.ds(pl.multiple_of(first + i * piece, piece), piece)

    def up_copy(d, hop, i, from_cache=False):
        src = cache.at[pl.ds(i * piece, piece)] if from_cache else window.at[d - hop, span(mine, i)]
        return remote(
            src,
            window.at[d, span(mine, i)],
            up_send.at[d, i],
            up_recv.at[d, i],
            {"tok": (tok + 2 * hop) % n_tok},
        )

    def side_copy(d, i, from_cache=False):
        src = cache.at[pl.ds(i * piece, piece)] if from_cache else window.at[d, span(mine, i)]
        return remote(
            src,
            window.at[d, span(mine, i)],
            side_send.at[d, i],
            side_recv.at[d, i],
            {"tok": sibling},
        )

    def side_arrival(d, i):
        dst = window.at[d, span(theirs, i)]
        return remote(dst, dst, side_send.at[d, i], side_recv.at[d, i], {"tok": sibling})

    for i in range(PIECES):
        side_copy(0, i, True).start()

        @pl.when(chip + 1 < chips)
        def _():
            up_copy(1, 1, i, True).start()

    for i in range(PIECES):

        @pl.when(chip + 3 < chips)
        def _():
            up_copy(3, 3, i, True).start()

    def own_copy(k):
        to = (place + k) % plane
        return remote(
            feat_own.at[(to % SEQS) % 2],
            feat_all.at[rank, x],
            own_send.at[k],
            feat_recv.at[rank, x],
            {"hs": half * plane + to},
        )

    def cross_copy(k):
        to = (place + k) % plane
        return remote(
            feat_cross.at[(to % SEQS) % 2],
            feat_all.at[other_rank, x],
            cross_send.at[k],
            feat_recv.at[other_rank, x],
            {"hs": half * plane + to},
        )

    def half_copy():
        return remote(feat_own, feat_cross, half_send, half_recv, {"hs": other_half})

    @pl.loop(1, plane)
    def _(k):
        own_copy(k).start()

    feat_all[rank, x] = feat_own[x % 2]

    if CROSS_AT == "start":
        half_copy().start()

    for i in range(PIECES):
        side_arrival(0, i).wait_recv()

    def stats_part(d, n):
        at = pl.ds(n * pair, pair)
        key_rows = window[d, :, 0:HD]
        value_rows = window[d, :, HD : 2 * HD]
        scores = lax.dot_general(
            key_rows, qs[at], CONTRACT_LAST, preferred_element_type=jnp.float32
        )
        dweights = lax.dot_general(
            value_rows, us[at], CONTRACT_LAST, preferred_element_type=jnp.float32
        )
        key_pos = (chip - d) * pair + lax.broadcasted_iota(jnp.int32, (pair, pair), 0)
        allowed = (key_pos <= position) & (key_pos >= start)
        scores = jnp.where(allowed, scores * (scale * LOG2E), NEG_FILL)
        top_old = row_top[:, at]
        top = jnp.maximum(top_old, jnp.max(scores, axis=0, keepdims=True))
        exp_terms = jnp.exp2(scores - top)
        factor = jnp.exp2(top_old - top)
        row_top[:, at] = top
        row_total[:, at] = row_total[:, at] * factor + jnp.sum(exp_terms, axis=0, keepdims=True)
        row_weighted[:, at] = row_weighted[:, at] * factor + jnp.sum(
            exp_terms * dweights, axis=0, keepdims=True
        )
        exps[d, :, at] = exp_terms
        dws[d, :, at] = dweights
        tops[d, :, at] = top

    def stats_block(d):
        @pl.when((chip >= d) & (d <= reach))
        def _():
            for n in range(n_pairs):
                stats_part(d, n)

    def passed_on(d, hop, next_hops):
        for i in range(PIECES):

            @pl.when((chip >= d) & (d <= reach))
            def _():
                up_copy(d, hop, i).wait_recv()
                side_copy(d, i).start()

            for hop_on in next_hops:

                @pl.when((chip >= d) & (d + hop_on <= reach) & (chip + hop_on < chips))
                def _():
                    up_copy(d + hop_on, hop_on, i).start()

    def joined(d):
        for i in range(PIECES):

            @pl.when((chip >= d) & (d <= reach))
            def _():
                side_arrival(d, i).wait_recv()

    @pl.loop(0, reach // 3 + 1)
    def _(turn):
        d = 3 * turn
        stats_block(d)
        passed_on(d + 1, 1, (1,))
        passed_on(d + 3, 3, (3, 1))
        joined(d + 1)
        stats_block(d + 1)
        passed_on(d + 2, 1, ())
        joined(d + 2)
        stats_block(d + 2)
        joined(d + 3)

    if CROSS_AT == "mid":
        half_copy().start()

    inverse = 1.0 / row_total[...]
    row_delta = stats.at[3:4]
    row_delta[...] = row_weighted[...] * inverse
    row_total[...] = inverse

    def grads_part(d, n):
        at = pl.ds(n * pair, pair)
        factor = jnp.exp2(tops[d, :, at] - row_top[:, at]) * row_total[:, at]
        weights = exps[d, :, at] * factor
        dscores = (weights * (dws[d, :, at] - row_delta[:, at])).astype(jnp.bfloat16)
        weights = weights.astype(jnp.bfloat16)
        key_rows = window[d, :, 0:HD]
        key_grads = jnp.dot(dscores, qs[at], preferred_element_type=jnp.float32)
        dvalues = jnp.dot(weights, us[at], preferred_element_type=jnp.float32)
        if n == 0:
            terms[:, 0:HD] = key_grads
            terms[:, HD : 2 * HD] = dvalues
        else:
            terms[:, 0:HD] += key_grads
            terms[:, HD : 2 * HD] += dvalues
        dq_acc[:, at] += lax.dot_general(
            key_rows, dscores, CONTRACT_FIRST, preferred_element_type=jnp.float32
        )

    def rows_of(i):
        return pl.ds(i * piece, piece)

    def back_copy(d, i):
        return remote(
            sib_out.at[d, rows_of(i)],
            sib_in.at[d, rows_of(i)],
            back_send.at[d, i],
            back_recv.at[d, i],
            {"tok": sibling},
        )

    def down_copy(d, hop, i):
        return remote(
            run_out.at[d, rows_of(i)],
            run_in.at[d, rows_of(i)],
            down_send.at[d, i],
            down_recv.at[d, i],
            {"tok": (tok + n_tok - 2 * hop) % n_tok},
        )

    def grads_block(d):
        @pl.when((chip >= d) & (d <= reach))
        def _():
            for n in range(n_pairs):
                grads_part(d, n)
            sent = terms[pl.ds(pl.multiple_of(theirs, rows), rows)]
            sib_out[d, :, 0:HD] = (sent[:, 0:HD] * scale).astype(jnp.bfloat16)
            sib_out[d, :, HD : 2 * HD] = sent[:, HD : 2 * HD].astype(jnp.bfloat16)
            for i in range(PIECES):
                back_copy(d, i).start()
            kept = terms[pl.ds(pl.multiple_of(mine, rows), rows)]
            own_terms[d, :, 0:HD] = kept[:, 0:HD] * scale
            own_terms[d, :, HD : 2 * HD] = kept[:, HD : 2 * HD]

    def summed(d, i, children):
        back_copy(d, i).wait_recv()
        own_terms[d, rows_of(i)] += sib_in[d, rows_of(i)].astype(jnp.float32)
        for child in children:

            @pl.when((d + child <= reach) & (chip + child < chips))
            def _():
                down_copy(d + child, child, i).wait_recv()
                own_terms[d, rows_of(i)] += run_in[d + child, rows_of(i)].astype(jnp.float32)

    def sent_down(d, hop, children):
        for i in range(PIECES):

            @pl.when((chip >= d) & (d <= reach))
            def _():
                summed(d, i, children)
                run_out[d, rows_of(i)] = own_terms[d, rows_of(i)].astype(jnp.bfloat16)
                down_copy(d, hop, i).start()

    @pl.loop(0, reach // 3 + 1)
    def _(turn):
        d = 3 * (reach // 3 - turn)
        grads_block(d + 2)
        grads_block(d + 1)
        sent_down(d + 4, 1, (1,))
        sent_down(d + 2, 1, ())
        sent_down(d + 6, 3, (1, 3))
        grads_block(d)

    for layer in range(layers):
        for head in range(heads):
            at = (layer * heads + head) * rows
            block = jnp.transpose(dq_acc[:, at : at + rows]) * scale
            query_grads[layer, :, head * HD : (head + 1) * HD] = block.astype(jnp.bfloat16)
    sent_down(1, 1, (1,))
    sent_down(3, 3, (1, 3))
    for i in range(PIECES):
        summed(0, i, (1, 3))

    for q in range(2):
        cut = own_terms[0, :, q * HD : (q + 1) * HD].astype(jnp.bfloat16)
        cache_grads[:, q * HD : (q + 1) * HD] = cut
        grads_out[q] = cut

    def grads_copy(k):
        to = (x + k) % SEQS
        return remote(
            grads_out.at[to // 2],
            grads_in.at[pl.ds(pl.multiple_of(x * rows, rows), rows)],
            grads_send.at[k],
            grads_recv.at[x],
            {"hs": hs - x + to},
        )

    def grads_arrival(k):
        came = (x + SEQS - k) % SEQS
        return remote(
            grads_out.at[0],
            grads_in.at[pl.ds(pl.multiple_of(came * rows, rows), rows)],
            grads_send.at[k],
            grads_recv.at[came],
            {"hs": hs},
        )

    for k in range(1, SEQS):
        grads_copy(k).start()
    grads_in[pl.ds(pl.multiple_of(x * rows, rows), rows)] = grads_out[x // 2]

    half_copy().wait_recv()

    @pl.loop(1, plane)
    def _(k):
        cross_copy(k).start()

    feat_all[other_rank, x] = feat_cross[x % 2]

    def feat_arrival(from_rank, k):
        came = (place + k) % plane
        came_rank = (from_rank // RANKS_Y) * RANKS_Y + came // SEQS
        dst = feat_all.at[came_rank, came % SEQS]
        return remote(
            dst, dst, own_send.at[k], feat_recv.at[came_rank, came % SEQS], {"hs": hs}
        )

    @pl.loop(1, plane)
    def _(k):
        feat_arrival(rank, k).wait_recv()

    for k in range(1, SEQS):
        grads_arrival(k).wait_recv()

    cut_rows = row_block // 2

    def product(r):
        block = jnp.zeros((2 * row_block, HD), jnp.float32)
        for s in range(SEQS):
            block += jnp.dot(
                feat_all[r, s],
                grads_in[s * rows : (s + 1) * rows],
                preferred_element_type=jnp.float32,
            )
        for j in range(2):
            u = 2 * r + j
            for c in range(2):
                first = j * row_block + c * cut_rows
                parts[c, u % GROUP, u // GROUP] = block[first : first + cut_rows]

    @pl.loop(0, RANKS_Y)
    def _(k):
        product(half * RANKS_Y + k)

    @pl.loop(1, plane)
    def _(k):
        feat_arrival(other_rank, k).wait_recv()

    @pl.loop(0, RANKS_Y)
    def _(k):
        product((1 - half) * RANKS_Y + k)

    def core_copy(v):
        return remote(
            near_out.at[1, v], core_in.at[v], core_send.at[v], core_recv.at[v], {"tok": sibling}
        )

    for k in (1, 2, 3, 0):
        v = (spot + k) % GROUP
        near_out[1, v] = parts[1 - core, v].astype(jnp.bfloat16)
        core_copy(v).start()

    def near_copy(k):
        v = (spot + k) % GROUP
        return remote(
            near_out.at[0, v],
            near_in.at[GROUP - k],
            near_send.at[k],
            near_recv.at[GROUP - k],
            {"tok": near_tok(k)},
        )

    for k in (1, 2, 3, 0):
        v = (spot + k) % GROUP
        core_copy(v).wait_recv()
        total = parts[core, v] + core_in[v].astype(jnp.float32)
        if k == 0:
            parts[core, v] = total
        else:
            near_out[0, v] = total.astype(jnp.bfloat16)
            near_copy(k).start()

    def near_arrival(k):
        return remote(
            near_out.at[0, spot], near_in.at[k], near_send.at[k], near_recv.at[k], {"tok": tok}
        )

    for k in range(1, GROUP):
        near_arrival(k).wait_recv()
        parts[core, spot] += near_in[k].astype(jnp.float32)

    def far_copy(k):
        return remote(
            far_out.at[k],
            far_in.at[GROUP - k],
            far_send.at[k],
            far_recv.at[GROUP - k],
            {"tok": far_tok(k)},
        )

    for k in range(1, GROUP):
        far_out[k] = parts[core, spot, (group + k) % GROUP].astype(jnp.bfloat16)
        far_copy(k).start()

    def far_arrival(k):
        return remote(far_out.at[k], far_in.at[k], far_send.at[k], far_recv.at[k], {"tok": tok})

    total = parts[core, spot, group]
    for k in range(1, GROUP):
        far_arrival(k).wait_recv()
        total = total + far_in[k].astype(jnp.float32)
    last_out[...] = total

    parity = x % 2
    owner = tok - core + parity
    same_core = core == parity

    def last_copy(to_hs, k):
        return remote(
            last_out, last_in.at[core], last_send.at[k], last_recv.at[core],
            {"hs": to_hs, "tok": owner},
        )

    last_copy(beside, 1).start()

    @pl.when(same_core)
    def _():
        last_in[core] = total

    @pl.when(jnp.logical_not(same_core))
    def _():
        last_copy(hs, 0).start()

    def last_arrival(c):
        return remote(
            last_out, last_in.at[c], last_send.at[0], last_recv.at[c], {"hs": hs, "tok": tok}
        )

    for c in range(2):

        @pl.when(jnp.logical_not(same_core & (core == c)))
        def _():
            last_arrival(c).wait_recv()

        block = last_in[c]
        width = weight_grads.shape[1]
        weight_grads[c * cut_rows : (c + 1) * cut_rows] = jnp.where(
            parity == 0, block[:, 0:width], block[:, width : 2 * width]
        )

    last_copy(beside, 1).wait_send()

    @pl.when(jnp.logical_not(same_core))
    def _():
        last_copy(hs, 0).wait_send()

    for k in range(1, GROUP):
        far_copy(k).wait_send()
        near_copy(k).wait_send()
        grads_copy(k).wait_send()
    for v in range(GROUP):
        core_copy(v).wait_send()
    half_copy().wait_send()

    @pl.loop(1, plane)
    def _(k):
        own_copy(k).wait_send()
        cross_copy(k).wait_send()

    @pl.loop(0, reach + 1)
    def _(d):
        for i in range(PIECES):

            @pl.when(chip >= d)
            def _():
                side_copy(d, i).wait_send()
                back_copy(d, i).wait_send()

            for last, hop in ((d % 3 != 0, 1), ((d % 3 == 0) & (d > 0), 3)):

                @pl.when((chip >= d) & last)
                def _():
                    down_copy(d, hop, i).wait_send()

                @pl.when((chip + hop >= d) & (chip + hop < chips) & last)
                def _():
                    up_copy(d, hop, i).wait_send()


def shards(queries, out_grads, kv_cache, features, doc_lens):
    layers, _, rows, columns = queries.shape
    feats = features.shape[2]
    n_tok = lax.axis_size("tok")
    slots = n_tok // 4 + 1
    n_rows = layers * columns // HD * rows
    pair = 2 * rows
    ranks = 2 * RANKS_Y
    cut = feats // 8
    vmem = pl.BlockSpec(memory_space=pltpu.VMEM)
    dma = pltpu.SemaphoreType.DMA
    sems = dma((slots, PIECES))
    block = (slots, rows, 2 * HD)
    bf16, f32 = jnp.bfloat16, jnp.float32
    query_grads, cache_grads, weight_grads = pl.pallas_call(
        functools.partial(kernel, n_tok),
        out_shape=(
            jax.ShapeDtypeStruct((layers, rows, columns), bf16),
            jax.ShapeDtypeStruct((rows, 2 * HD), bf16),
            jax.ShapeDtypeStruct((feats // 4, 2 * HD // SEQS), f32),
        ),
        in_specs=[pl.BlockSpec(memory_space=pltpu.SMEM), vmem, vmem, vmem, vmem],
        out_specs=(vmem, vmem, vmem),
        scratch_shapes=[
            pltpu.VMEM((n_rows, HD), bf16),
            pltpu.VMEM((n_rows, HD), bf16),
            pltpu.VMEM((slots, pair, 2 * HD), bf16),
            pltpu.VMEM((slots, pair, n_rows), f32),
            pltpu.VMEM((slots, pair, n_rows), f32),
            pltpu.VMEM((slots, 1, n_rows), f32),
            pltpu.VMEM((8, n_rows), f32),
            pltpu.VMEM((HD, n_rows), f32),
            pltpu.VMEM((pair, 2 * HD), f32),
            pltpu.VMEM(block, f32),
            pltpu.VMEM(block, bf16),
            pltpu.VMEM(block, bf16),
            pltpu.VMEM(block, bf16),
            pltpu.VMEM(block, bf16),
            pltpu.VMEM((2, feats // 2, rows), bf16),
            pltpu.VMEM((2, feats // 2, rows), bf16),
            pltpu.VMEM((ranks, SEQS, feats // 2, rows), bf16),
            pltpu.VMEM((2, rows, HD), bf16),
            pltpu.VMEM((SEQS * rows, HD), bf16),
            pltpu.VMEM((2, GROUP, GROUP, cut, HD), f32),
            pltpu.VMEM((GROUP, GROUP, cut, HD), bf16),
            pltpu.VMEM((2, GROUP, GROUP, cut, HD), bf16),
            pltpu.VMEM((GROUP, GROUP, cut, HD), bf16),
            pltpu.VMEM((GROUP, cut, HD), bf16),
            pltpu.VMEM((GROUP, cut, HD), bf16),
            pltpu.VMEM((cut, HD), f32),
            pltpu.VMEM((2, cut, HD), f32),
        ]
        + [sems] * 8
        + [dma((16,)), dma((16,)), dma((ranks, SEQS)), dma, dma]
        + [dma((4,))] * 8
        + [dma((2,))] * 2,
        compiler_params=pltpu.CompilerParams(
            collective_id=0, has_side_effects=True, vmem_limit_bytes=48 * 2**20
        ),
        name="backward",
    )(doc_lens, queries[:, 0], out_grads[:, 0], kv_cache[0], features[0])
    return (query_grads[:, None], cache_grads[None], weight_grads)


def solution(mesh):
    placed = (
        P(None, "hs", "tok", None),
        P(None, "hs", "tok", None),
        P("hs", "tok", None),
        P("hs", "tok", None),
        P(),
    )
    return jax.shard_map(
        shards,
        mesh=mesh,
        in_specs=placed,
        out_specs=(P(None, "hs", "tok", None), P("hs", "tok", None), P("tok", "hs")),
        check_vma=False,
    )
```

```python
import functools

import jax
import jax.numpy as jnp
from jax import lax
from jax.experimental import pallas as pl
from jax.experimental.pallas import tpu as pltpu
from jax.sharding import PartitionSpec as P

HD = 128
SEQS = 4
RANKS_Y = 4
GROUP = 4
NEG_FILL = -1e30
PIECES = 2
LOG2E = 1.4426950408889634
MESH = pl.DeviceIdType.MESH
CONTRACT_LAST = (((1,), (1,)), ((), ()))
CONTRACT_FIRST = (((0,), (0,)), ((), ()))


def remote(src, dst, send_sem, recv_sem, device):
    return pltpu.make_async_remote_copy(
        src_ref=src,
        dst_ref=dst,
        send_sem=send_sem,
        recv_sem=recv_sem,
        device_id=device,
        device_id_type=MESH,
    )


def kernel(
    n_tok,
    doc_lens,
    queries,
    upstream,
    cache,
    features,
    query_grads,
    cache_grads,
    weight_grads,
    qs,
    us,
    window,
    exps,
    dws,
    tops,
    stats,
    dq_acc,
    terms,
    own_terms,
    sib_out,
    sib_in,
    run_out,
    run_in,
    feat_in,
    feat_own,
    feat_relay,
    feat_cross,
    feat_all,
    grads_out,
    grads_in,
    parts,
    core_in,
    near_out,
    near_in,
    far_out,
    far_in,
    last_out,
    last_in,
    up_send,
    up_recv,
    side_send,
    side_recv,
    back_send,
    back_recv,
    down_send,
    down_recv,
    own_send,
    cross_send,
    feat_recv,
    leg_send,
    leg_recv,
    load_sems,
    grads_send,
    grads_recv,
    core_send,
    core_recv,
    near_send,
    near_recv,
    far_send,
    far_recv,
    last_send,
    last_recv,
):
    layers, rows, columns = queries.shape
    heads = columns // HD
    n_rows = layers * heads * rows
    chips = n_tok // 2
    reach = n_tok // 4
    piece = rows // PIECES
    pair = 2 * rows
    n_pairs = n_rows // pair
    scale = HD ** (-0.5)

    tok = lax.axis_index("tok")
    hs = lax.axis_index("hs")
    chip = tok // 2
    core = tok % 2
    sibling = tok + 1 - 2 * core
    mine = core * rows
    theirs = (1 - core) * rows
    x = hs % SEQS
    y = (hs // SEQS) % RANKS_Y
    plane = SEQS * RANKS_Y
    half = hs // plane
    place = hs % plane
    rank = half * RANKS_Y + y
    upper = chip // (chips // 2)
    opposite = (tok + n_tok // 2) % n_tok
    kept_half = half * plane + place
    other_half = (1 - half) * plane + place
    leg_hs = (
        kept_half * upper + other_half * (1 - upper),
        kept_half * (1 - upper) + other_half * upper,
    )
    other_rank = (1 - half) * RANKS_Y + y
    beside = hs + 1 - 2 * (x % 2)
    spot = chip % GROUP
    group = chip // GROUP

    def near_tok(k):
        return (group * GROUP + (spot + k) % GROUP) * 2 + core

    def far_tok(k):
        return (((group + k) % GROUP) * GROUP + spot) * 2 + core

    def plane_hs(k):
        return half * plane + (place + k) % plane

    barrier = pltpu.get_barrier_semaphore()
    met = [{"tok": sibling}]
    met += [{"tok": near_tok(k)} for k in range(1, GROUP)]
    met += [{"tok": far_tok(k)} for k in range(1, GROUP)]
    met += [{"hs": plane_hs(k)} for k in range(1, plane)]
    met += [{"hs": leg_hs[0], "tok": opposite}, {"hs": leg_hs[1], "tok": opposite}]
    met += [{"hs": beside, "tok": sibling}]
    expected = len(met)
    for k in (1, 3):

        @pl.when(chip + k < chips)
        def _():
            pl.semaphore_signal(
                barrier, inc=1, device_id={"tok": (tok + 2 * k) % n_tok}, device_id_type=MESH
            )

        @pl.when(chip >= k)
        def _():
            pl.semaphore_signal(
                barrier,
                inc=1,
                device_id={"tok": (tok + n_tok - 2 * k) % n_tok},
                device_id_type=MESH,
            )

        expected = expected + (2 * chips - 1 - k - chip) // chips + (chip + chips - k) // chips
    for device in met:
        pl.semaphore_signal(barrier, inc=1, device_id=device, device_id_type=MESH)

    loads = [
        pltpu.make_async_copy(
            cache, window.at[0, pl.ds(pl.multiple_of(mine, rows), rows)], load_sems.at[0]
        ),
        pltpu.make_async_copy(features, feat_in, load_sems.at[1]),
    ]
    for layer in range(layers):
        for head in range(heads):
            at = (layer * heads + head) * rows
            for source, target in ((queries, qs), (upstream, us)):
                loads.append(
                    pltpu.make_async_copy(
                        source.at[layer, :, head * HD : (head + 1) * HD],
                        target.at[at : at + rows],
                        load_sems.at[len(loads)],
                    )
                )
    for load in loads:
        load.start()
    loads[1].wait()

    row_block = feat_in.shape[1] // 4
    for n in range(feat_in.shape[1] // HD):
        turned = jnp.transpose(feat_in[:, n * HD : (n + 1) * HD].astype(jnp.float32)).astype(
            jnp.bfloat16
        )
        first = n * HD
        while first < (n + 1) * HD:
            block = first // row_block
            last = min((block + 1) * row_block, (n + 1) * HD)
            to = (block // 2) * row_block + first - block * row_block
            feat_own[block % 2, to : to + last - first] = turned[
                first - n * HD : last - n * HD
            ]
            first = last

    row_top = stats.at[0:1]
    row_total = stats.at[1:2]
    row_weighted = stats.at[2:3]
    row_top[...] = jnp.full((1, n_rows), NEG_FILL, jnp.float32)
    row_total[...] = jnp.zeros((1, n_rows), jnp.float32)
    row_weighted[...] = jnp.zeros((1, n_rows), jnp.float32)
    dq_acc[...] = jnp.zeros_like(dq_acc)

    seq = x
    position = tok * rows + lax.rem(lax.broadcasted_iota(jnp.int32, (1, pair), 1), rows)
    start = jnp.zeros((1, pair), jnp.int32)
    end = jnp.int32(0)
    for k in range(doc_lens.shape[1] - 1):
        end = end + doc_lens[seq, k]
        start = jnp.where(position >= end, end, start)

    loads[0].wait()
    pl.semaphore_wait(barrier, expected)

    def span(first, i):
        return pl.ds(pl.multiple_of(first + i * piece, piece), piece)

    def up_copy(d, hop, i):
        return remote(
            window.at[d - hop, span(mine, i)],
            window.at[d, span(mine, i)],
            up_send.at[d, i],
            up_recv.at[d, i],
            {"tok": (tok + 2 * hop) % n_tok},
        )

    def side_copy(d, i):
        return remote(
            window.at[d, span(mine, i)],
            window.at[d, span(mine, i)],
            side_send.at[d, i],
            side_recv.at[d, i],
            {"tok": sibling},
        )

    def side_arrival(d, i):
        dst = window.at[d, span(theirs, i)]
        return remote(dst, dst, side_send.at[d, i], side_recv.at[d, i], {"tok": sibling})

    for i in range(PIECES):
        side_copy(0, i).start()

        @pl.when(chip + 1 < chips)
        def _():
            up_copy(1, 1, i).start()

    for i in range(PIECES):

        @pl.when(chip + 3 < chips)
        def _():
            up_copy(3, 3, i).start()

    def own_copy(k):
        to = (place + k) % plane
        return remote(
            feat_own.at[(to % SEQS) % 2],
            feat_all.at[rank, x],
            own_send.at[k],
            feat_recv.at[rank, x],
            {"hs": half * plane + to},
        )

    def cross_copy(k):
        to = (place + k) % plane
        return remote(
            feat_cross.at[(to % SEQS) % 2],
            feat_all.at[other_rank, x],
            cross_send.at[k],
            feat_recv.at[other_rank, x],
            {"hs": half * plane + to},
        )

    def leg_copy(leg, p):
        source, target = ((feat_own, feat_relay), (feat_relay, feat_cross))[leg]
        return remote(
            source.at[p],
            target.at[p],
            leg_send.at[leg, p],
            leg_recv.at[leg, p],
            {"hs": leg_hs[p], "tok": opposite},
        )

    def spread(p):
        first = (p + place) % 2

        @pl.loop(0, plane // 2)
        def _(m):
            @pl.when(first + 2 * m > 0)
            def _():
                cross_copy(first + 2 * m).start()

    leg_copy(0, 0).start()

    @pl.loop(1, plane)
    def _(k):
        own_copy(k).start()

    feat_all[rank, x] = feat_own[x % 2]

    for load in loads[2:]:
        load.wait()

    for i in range(PIECES):
        side_arrival(0, i).wait_recv()

    def stats_part(d, n):
        at = pl.ds(n * pair, pair)
        key_rows = window[d, :, 0:HD]
        value_rows = window[d, :, HD : 2 * HD]
        scores = lax.dot_general(
            key_rows, qs[at], CONTRACT_LAST, preferred_element_type=jnp.float32
        )
        dweights = lax.dot_general(
            value_rows, us[at], CONTRACT_LAST, preferred_element_type=jnp.float32
        )
        key_pos = (chip - d) * pair + lax.broadcasted_iota(jnp.int32, (pair, pair), 0)
        allowed = (key_pos <= position) & (key_pos >= start)
        scores = jnp.where(allowed, scores * (scale * LOG2E), NEG_FILL)
        top_old = row_top[:, at]
        top = jnp.maximum(top_old, jnp.max(scores, axis=0, keepdims=True))
        exp_terms = jnp.exp2(scores - top)
        factor = jnp.exp2(top_old - top)
        row_top[:, at] = top
        row_total[:, at] = row_total[:, at] * factor + jnp.sum(exp_terms, axis=0, keepdims=True)
        row_weighted[:, at] = row_weighted[:, at] * factor + jnp.sum(
            exp_terms * dweights, axis=0, keepdims=True
        )
        exps[d, :, at] = exp_terms
        dws[d, :, at] = dweights
        tops[d, :, at] = top

    def stats_block(d):
        @pl.when((chip >= d) & (d <= reach))
        def _():
            for n in range(n_pairs):
                stats_part(d, n)

    def passed_on(d, hop, next_hops):
        for i in range(PIECES):

            @pl.when((chip >= d) & (d <= reach))
            def _():
                up_copy(d, hop, i).wait_recv()
                side_copy(d, i).start()

            for hop_on in next_hops:

                @pl.when((chip >= d) & (d + hop_on <= reach) & (chip + hop_on < chips))
                def _():
                    up_copy(d + hop_on, hop_on, i).start()

    def joined(d):
        for i in range(PIECES):

            @pl.when((chip >= d) & (d <= reach))
            def _():
                side_arrival(d, i).wait_recv()

    @pl.loop(0, reach // 3 + 1)
    def _(turn):
        d = 3 * turn

        @pl.when(turn == 1)
        def _():
            leg_copy(0, 1).start()

        @pl.when(turn == 2)
        def _():
            leg_copy(0, 0).wait_recv()
            leg_copy(1, 0).start()

        stats_block(d)
        passed_on(d + 1, 1, (1,))
        passed_on(d + 3, 3, (3, 1))
        joined(d + 1)
        stats_block(d + 1)
        passed_on(d + 2, 1, ())
        joined(d + 2)
        stats_block(d + 2)
        joined(d + 3)

    leg_copy(0, 1).wait_recv()
    leg_copy(1, 1).start()

    inverse = 1.0 / row_total[...]
    row_delta = stats.at[3:4]
    row_delta[...] = row_weighted[...] * inverse
    row_total[...] = inverse

    def grads_part(d, n):
        at = pl.ds(n * pair, pair)
        factor = jnp.exp2(tops[d, :, at] - row_top[:, at]) * row_total[:, at]
        weights = exps[d, :, at] * factor
        dscores = (weights * (dws[d, :, at] - row_delta[:, at])).astype(jnp.bfloat16)
        weights = weights.astype(jnp.bfloat16)
        key_rows = window[d, :, 0:HD]
        key_grads = jnp.dot(dscores, qs[at], preferred_element_type=jnp.float32)
        dvalues = jnp.dot(weights, us[at], preferred_element_type=jnp.float32)
        if n == 0:
            terms[:, 0:HD] = key_grads
            terms[:, HD : 2 * HD] = dvalues
        else:
            terms[:, 0:HD] += key_grads
            terms[:, HD : 2 * HD] += dvalues
        dq_acc[:, at] += lax.dot_general(
            key_rows, dscores, CONTRACT_FIRST, preferred_element_type=jnp.float32
        )

    def rows_of(i):
        return pl.ds(i * piece, piece)

    def back_copy(d, i):
        return remote(
            sib_out.at[d, rows_of(i)],
            sib_in.at[d, rows_of(i)],
            back_send.at[d, i],
            back_recv.at[d, i],
            {"tok": sibling},
        )

    def down_copy(d, hop, i):
        return remote(
            run_out.at[d, rows_of(i)],
            run_in.at[d, rows_of(i)],
            down_send.at[d, i],
            down_recv.at[d, i],
            {"tok": (tok + n_tok - 2 * hop) % n_tok},
        )

    def grads_block(d):
        @pl.when((chip >= d) & (d <= reach))
        def _():
            for n in range(n_pairs):
                grads_part(d, n)
            sent = terms[pl.ds(pl.multiple_of(theirs, rows), rows)]
            sib_out[d, :, 0:HD] = (sent[:, 0:HD] * scale).astype(jnp.bfloat16)
            sib_out[d, :, HD : 2 * HD] = sent[:, HD : 2 * HD].astype(jnp.bfloat16)
            for i in range(PIECES):
                back_copy(d, i).start()
            kept = terms[pl.ds(pl.multiple_of(mine, rows), rows)]
            own_terms[d, :, 0:HD] = kept[:, 0:HD] * scale
            own_terms[d, :, HD : 2 * HD] = kept[:, HD : 2 * HD]

    def summed(d, i, children):
        back_copy(d, i).wait_recv()
        own_terms[d, rows_of(i)] += sib_in[d, rows_of(i)].astype(jnp.float32)
        for child in children:

            @pl.when((d + child <= reach) & (chip + child < chips))
            def _():
                down_copy(d + child, child, i).wait_recv()
                own_terms[d, rows_of(i)] += run_in[d + child, rows_of(i)].astype(jnp.float32)

    def sent_down(d, hop, children):
        for i in range(PIECES):

            @pl.when((chip >= d) & (d <= reach))
            def _():
                summed(d, i, children)
                run_out[d, rows_of(i)] = own_terms[d, rows_of(i)].astype(jnp.bfloat16)
                down_copy(d, hop, i).start()

    @pl.loop(0, reach // 3 + 1)
    def _(turn):
        d = 3 * (reach // 3 - turn)
        grads_block(d + 2)
        grads_block(d + 1)
        sent_down(d + 4, 1, (1,))
        sent_down(d + 2, 1, ())
        sent_down(d + 6, 3, (1, 3))
        grads_block(d)

        @pl.when(turn == 1)
        def _():
            leg_copy(1, 0).wait_recv()
            spread(0)

    for layer in range(layers):
        for head in range(heads):
            at = (layer * heads + head) * rows
            block = jnp.transpose(dq_acc[:, at : at + rows]) * scale
            query_grads[layer, :, head * HD : (head + 1) * HD] = block.astype(jnp.bfloat16)
    sent_down(1, 1, (1,))
    sent_down(3, 3, (1, 3))
    leg_copy(1, 1).wait_recv()
    spread(1)
    feat_all[other_rank, x] = feat_cross[x % 2]
    for i in range(PIECES):
        summed(0, i, (1, 3))

    for q in range(2):
        cut = own_terms[0, :, q * HD : (q + 1) * HD].astype(jnp.bfloat16)
        cache_grads[:, q * HD : (q + 1) * HD] = cut
        grads_out[q] = cut

    def grads_copy(k):
        to = (x + k) % SEQS
        return remote(
            grads_out.at[to // 2],
            grads_in.at[pl.ds(pl.multiple_of(x * rows, rows), rows)],
            grads_send.at[k],
            grads_recv.at[x],
            {"hs": hs - x + to},
        )

    def grads_arrival(k):
        came = (x + SEQS - k) % SEQS
        return remote(
            grads_out.at[0],
            grads_in.at[pl.ds(pl.multiple_of(came * rows, rows), rows)],
            grads_send.at[k],
            grads_recv.at[came],
            {"hs": hs},
        )

    for k in range(1, SEQS):
        grads_copy(k).start()
    grads_in[pl.ds(pl.multiple_of(x * rows, rows), rows)] = grads_out[x // 2]

    def feat_arrival(from_rank, k):
        came = (place + k) % plane
        came_rank = (from_rank // RANKS_Y) * RANKS_Y + came // SEQS
        dst = feat_all.at[came_rank, came % SEQS]
        return remote(
            dst, dst, own_send.at[k], feat_recv.at[came_rank, came % SEQS], {"hs": hs}
        )

    @pl.loop(1, plane)
    def _(k):
        feat_arrival(rank, k).wait_recv()

    for k in range(1, SEQS):
        grads_arrival(k).wait_recv()

    cut_rows = row_block // 2

    def product(r):
        block = jnp.zeros((2 * row_block, HD), jnp.float32)
        for s in range(SEQS):
            block += jnp.dot(
                feat_all[r, s],
                grads_in[s * rows : (s + 1) * rows],
                preferred_element_type=jnp.float32,
            )
        for j in range(2):
            u = 2 * r + j
            for c in range(2):
                first = j * row_block + c * cut_rows
                parts[c, u % GROUP, u // GROUP] = block[first : first + cut_rows]

    @pl.loop(0, RANKS_Y)
    def _(k):
        product(half * RANKS_Y + k)

    @pl.loop(1, plane)
    def _(k):
        feat_arrival(other_rank, k).wait_recv()

    @pl.loop(0, RANKS_Y)
    def _(k):
        product((1 - half) * RANKS_Y + k)

    def core_copy(v):
        return remote(
            near_out.at[1, v], core_in.at[v], core_send.at[v], core_recv.at[v], {"tok": sibling}
        )

    for k in (1, 2, 3, 0):
        v = (spot + k) % GROUP
        near_out[1, v] = parts[1 - core, v].astype(jnp.bfloat16)
        core_copy(v).start()

    def near_copy(k):
        v = (spot + k) % GROUP
        return remote(
            near_out.at[0, v],
            near_in.at[GROUP - k],
            near_send.at[k],
            near_recv.at[GROUP - k],
            {"tok": near_tok(k)},
        )

    for k in (1, 2, 3, 0):
        v = (spot + k) % GROUP
        core_copy(v).wait_recv()
        total = parts[core, v] + core_in[v].astype(jnp.float32)
        if k == 0:
            parts[core, v] = total
        else:
            near_out[0, v] = total.astype(jnp.bfloat16)
            near_copy(k).start()

    def near_arrival(k):
        return remote(
            near_out.at[0, spot], near_in.at[k], near_send.at[k], near_recv.at[k], {"tok": tok}
        )

    for k in range(1, GROUP):
        near_arrival(k).wait_recv()
        parts[core, spot] += near_in[k].astype(jnp.float32)

    def far_copy(k):
        return remote(
            far_out.at[k],
            far_in.at[GROUP - k],
            far_send.at[k],
            far_recv.at[GROUP - k],
            {"tok": far_tok(k)},
        )

    for k in range(1, GROUP):
        far_out[k] = parts[core, spot, (group + k) % GROUP].astype(jnp.bfloat16)
        far_copy(k).start()

    def far_arrival(k):
        return remote(far_out.at[k], far_in.at[k], far_send.at[k], far_recv.at[k], {"tok": tok})

    total = parts[core, spot, group]
    for k in range(1, GROUP):
        far_arrival(k).wait_recv()
        total = total + far_in[k].astype(jnp.float32)
    last_out[...] = total

    parity = x % 2
    owner = tok - core + parity
    same_core = core == parity

    def last_copy(to_hs, k):
        return remote(
            last_out, last_in.at[core], last_send.at[k], last_recv.at[core],
            {"hs": to_hs, "tok": owner},
        )

    last_copy(beside, 1).start()

    @pl.when(same_core)
    def _():
        last_in[core] = total

    @pl.when(jnp.logical_not(same_core))
    def _():
        last_copy(hs, 0).start()

    def last_arrival(c):
        return remote(
            last_out, last_in.at[c], last_send.at[0], last_recv.at[c], {"hs": hs, "tok": tok}
        )

    for c in range(2):

        @pl.when(jnp.logical_not(same_core & (core == c)))
        def _():
            last_arrival(c).wait_recv()

        block = last_in[c]
        width = weight_grads.shape[1]
        weight_grads[c * cut_rows : (c + 1) * cut_rows] = jnp.where(
            parity == 0, block[:, 0:width], block[:, width : 2 * width]
        )

    last_copy(beside, 1).wait_send()

    @pl.when(jnp.logical_not(same_core))
    def _():
        last_copy(hs, 0).wait_send()

    for k in range(1, GROUP):
        far_copy(k).wait_send()
        near_copy(k).wait_send()
        grads_copy(k).wait_send()
    for v in range(GROUP):
        core_copy(v).wait_send()
    for leg in range(2):
        for p in range(2):
            leg_copy(leg, p).wait_send()

    @pl.loop(1, plane)
    def _(k):
        own_copy(k).wait_send()
        cross_copy(k).wait_send()

    @pl.loop(0, reach + 1)
    def _(d):
        for i in range(PIECES):

            @pl.when(chip >= d)
            def _():
                side_copy(d, i).wait_send()
                back_copy(d, i).wait_send()

            for last, hop in ((d % 3 != 0, 1), ((d % 3 == 0) & (d > 0), 3)):

                @pl.when((chip >= d) & last)
                def _():
                    down_copy(d, hop, i).wait_send()

                @pl.when((chip + hop >= d) & (chip + hop < chips) & last)
                def _():
                    up_copy(d, hop, i).wait_send()


def shards(queries, out_grads, kv_cache, features, doc_lens):
    layers, _, rows, columns = queries.shape
    feats = features.shape[2]
    n_tok = lax.axis_size("tok")
    slots = n_tok // 4 + 1
    n_rows = layers * columns // HD * rows
    pair = 2 * rows
    ranks = 2 * RANKS_Y
    cut = feats // 8
    vmem = pl.BlockSpec(memory_space=pltpu.VMEM)
    dma = pltpu.SemaphoreType.DMA
    sems = dma((slots, PIECES))
    block = (slots, rows, 2 * HD)
    bf16, f32 = jnp.bfloat16, jnp.float32
    query_grads, cache_grads, weight_grads = pl.pallas_call(
        functools.partial(kernel, n_tok),
        out_shape=(
            jax.ShapeDtypeStruct((layers, rows, columns), bf16),
            jax.ShapeDtypeStruct((rows, 2 * HD), bf16),
            jax.ShapeDtypeStruct((feats // 4, 2 * HD // SEQS), f32),
        ),
        in_specs=[pl.BlockSpec(memory_space=pltpu.SMEM)] + [pl.BlockSpec(memory_space=pl.ANY)] * 4,
        out_specs=(vmem, vmem, vmem),
        scratch_shapes=[
            pltpu.VMEM((n_rows, HD), bf16),
            pltpu.VMEM((n_rows, HD), bf16),
            pltpu.VMEM((slots, pair, 2 * HD), bf16),
            pltpu.VMEM((slots, pair, n_rows), f32),
            pltpu.VMEM((slots, pair, n_rows), f32),
            pltpu.VMEM((slots, 1, n_rows), f32),
            pltpu.VMEM((8, n_rows), f32),
            pltpu.VMEM((HD, n_rows), f32),
            pltpu.VMEM((pair, 2 * HD), f32),
            pltpu.VMEM(block, f32),
            pltpu.VMEM(block, bf16),
            pltpu.VMEM(block, bf16),
            pltpu.VMEM(block, bf16),
            pltpu.VMEM(block, bf16),
            pltpu.VMEM((rows, feats), bf16),
            pltpu.VMEM((2, feats // 2, rows), bf16),
            pltpu.VMEM((2, feats // 2, rows), bf16),
            pltpu.VMEM((2, feats // 2, rows), bf16),
            pltpu.VMEM((ranks, SEQS, feats // 2, rows), bf16),
            pltpu.VMEM((2, rows, HD), bf16),
            pltpu.VMEM((SEQS * rows, HD), bf16),
            pltpu.VMEM((2, GROUP, GROUP, cut, HD), f32),
            pltpu.VMEM((GROUP, GROUP, cut, HD), bf16),
            pltpu.VMEM((2, GROUP, GROUP, cut, HD), bf16),
            pltpu.VMEM((GROUP, GROUP, cut, HD), bf16),
            pltpu.VMEM((GROUP, cut, HD), bf16),
            pltpu.VMEM((GROUP, cut, HD), bf16),
            pltpu.VMEM((cut, HD), f32),
            pltpu.VMEM((2, cut, HD), f32),
        ]
        + [sems] * 8
        + [dma((16,)), dma((16,)), dma((ranks, SEQS)), dma((2, 2)), dma((2, 2))]
        + [dma((2 + 2 * layers * columns // HD,))]
        + [dma((4,))] * 8
        + [dma((2,))] * 2,
        compiler_params=pltpu.CompilerParams(
            collective_id=0, has_side_effects=True, vmem_limit_bytes=60 * 2**20
        ),
        name="backward",
    )(doc_lens, queries[:, 0], out_grads[:, 0], kv_cache[0], features[0])
    return (query_grads[:, None], cache_grads[None], weight_grads)


def solution(mesh):
    placed = (
        P(None, "hs", "tok", None),
        P(None, "hs", "tok", None),
        P("hs", "tok", None),
        P("hs", "tok", None),
        P(),
    )
    return jax.shard_map(
        shards,
        mesh=mesh,
        in_specs=placed,
        out_specs=(P(None, "hs", "tok", None), P("hs", "tok", None), P("tok", "hs")),
        check_vma=False,
    )
```

```python
import functools

import jax
import jax.numpy as jnp
from jax import lax
from jax.experimental import pallas as pl
from jax.experimental.pallas import tpu as pltpu
from jax.sharding import PartitionSpec as P

HD = 128
SEQS = 4
RANKS_Y = 4
GROUP = 4
NEG_FILL = -1e30
PIECES = 2
LOG2E = 1.4426950408889634
MESH = pl.DeviceIdType.MESH
CONTRACT_LAST = (((1,), (1,)), ((), ()))
CONTRACT_FIRST = (((0,), (0,)), ((), ()))


def remote(src, dst, send_sem, recv_sem, device):
    return pltpu.make_async_remote_copy(
        src_ref=src,
        dst_ref=dst,
        send_sem=send_sem,
        recv_sem=recv_sem,
        device_id=device,
        device_id_type=MESH,
    )


def kernel(
    n_tok,
    doc_lens,
    queries,
    upstream,
    cache,
    features,
    query_grads,
    cache_grads,
    weight_grads,
    qs,
    us,
    window,
    exps,
    dws,
    tops,
    stats,
    dq_acc,
    terms,
    own_terms,
    sib_out,
    sib_in,
    run_out,
    run_in,
    feat_in,
    feat_own,
    feat_relay,
    feat_cross,
    feat_all,
    grads_out,
    grads_in,
    parts,
    core_in,
    near_out,
    near_in,
    far_out,
    far_in,
    last_out,
    last_in,
    up_send,
    up_recv,
    side_send,
    side_recv,
    back_send,
    back_recv,
    down_send,
    down_recv,
    own_send,
    cross_send,
    feat_recv,
    leg_send,
    leg_recv,
    load_sems,
    grads_send,
    grads_recv,
    core_send,
    core_recv,
    near_send,
    near_recv,
    far_send,
    far_recv,
    last_send,
    last_recv,
):
    layers, rows, columns = queries.shape
    heads = columns // HD
    n_rows = layers * heads * rows
    chips = n_tok // 2
    reach = n_tok // 4
    piece = rows // PIECES
    pair = 2 * rows
    n_pairs = n_rows // pair
    scale = HD ** (-0.5)

    tok = lax.axis_index("tok")
    hs = lax.axis_index("hs")
    chip = tok // 2
    core = tok % 2
    sibling = tok + 1 - 2 * core
    mine = core * rows
    theirs = (1 - core) * rows
    x = hs % SEQS
    y = (hs // SEQS) % RANKS_Y
    plane = SEQS * RANKS_Y
    half = hs // plane
    place = hs % plane
    rank = half * RANKS_Y + y
    upper = chip // (chips // 2)
    opposite = (tok + n_tok // 2) % n_tok
    kept_half = half * plane + place
    other_half = (1 - half) * plane + place
    leg_hs = (
        kept_half * upper + other_half * (1 - upper),
        kept_half * (1 - upper) + other_half * upper,
    )
    other_rank = (1 - half) * RANKS_Y + y
    beside = hs + 1 - 2 * (x % 2)
    spot = chip % GROUP
    group = chip // GROUP

    def near_tok(k):
        return (group * GROUP + (spot + k) % GROUP) * 2 + core

    def far_tok(k):
        return (((group + k) % GROUP) * GROUP + spot) * 2 + core

    def plane_hs(k):
        return half * plane + (place + k) % plane

    barrier = pltpu.get_barrier_semaphore()
    met = [{"tok": sibling}]
    met += [{"tok": near_tok(k)} for k in range(1, GROUP)]
    met += [{"tok": far_tok(k)} for k in range(1, GROUP)]
    met += [{"hs": plane_hs(k)} for k in range(1, plane)]
    met += [{"hs": leg_hs[0], "tok": opposite}, {"hs": leg_hs[1], "tok": opposite}]
    met += [{"hs": beside, "tok": sibling}]
    expected = len(met)
    for k in (1, 3):

        @pl.when(chip + k < chips)
        def _():
            pl.semaphore_signal(
                barrier, inc=1, device_id={"tok": (tok + 2 * k) % n_tok}, device_id_type=MESH
            )

        @pl.when(chip >= k)
        def _():
            pl.semaphore_signal(
                barrier,
                inc=1,
                device_id={"tok": (tok + n_tok - 2 * k) % n_tok},
                device_id_type=MESH,
            )

        expected = expected + (2 * chips - 1 - k - chip) // chips + (chip + chips - k) // chips
    for device in met:
        pl.semaphore_signal(barrier, inc=1, device_id=device, device_id_type=MESH)

    loads = [
        pltpu.make_async_copy(
            cache, window.at[0, pl.ds(pl.multiple_of(mine, rows), rows)], load_sems.at[0]
        ),
        pltpu.make_async_copy(features, feat_in, load_sems.at[1]),
    ]
    for layer in range(layers):
        for head in range(heads):
            at = (layer * heads + head) * rows
            for source, target in ((queries, qs), (upstream, us)):
                loads.append(
                    pltpu.make_async_copy(
                        source.at[layer, :, head * HD : (head + 1) * HD],
                        target.at[at : at + rows],
                        load_sems.at[len(loads)],
                    )
                )
    for load in loads:
        load.start()
    loads[1].wait()

    row_block = feat_in.shape[1] // 4
    for n in range(feat_in.shape[1] // HD):
        turned = jnp.transpose(feat_in[:, n * HD : (n + 1) * HD].astype(jnp.float32)).astype(
            jnp.bfloat16
        )
        first = n * HD
        while first < (n + 1) * HD:
            block = first // row_block
            last = min((block + 1) * row_block, (n + 1) * HD)
            to = (block // 2) * row_block + first - block * row_block
            feat_own[block % 2, to : to + last - first] = turned[
                first - n * HD : last - n * HD
            ]
            first = last

    row_top = stats.at[0:1]
    row_total = stats.at[1:2]
    row_weighted = stats.at[2:3]
    row_top[...] = jnp.full((1, n_rows), NEG_FILL, jnp.float32)
    row_total[...] = jnp.zeros((1, n_rows), jnp.float32)
    row_weighted[...] = jnp.zeros((1, n_rows), jnp.float32)
    dq_acc[...] = jnp.zeros_like(dq_acc)

    seq = x
    position = tok * rows + lax.rem(lax.broadcasted_iota(jnp.int32, (1, pair), 1), rows)
    start = jnp.zeros((1, pair), jnp.int32)
    end = jnp.int32(0)
    for k in range(doc_lens.shape[1] - 1):
        end = end + doc_lens[seq, k]
        start = jnp.where(position >= end, end, start)

    loads[0].wait()
    pl.semaphore_wait(barrier, expected)

    def span(first, i):
        return pl.ds(pl.multiple_of(first + i * piece, piece), piece)

    def up_copy(d, hop, i):
        return remote(
            window.at[d - hop, span(mine, i)],
            window.at[d, span(mine, i)],
            up_send.at[d, i],
            up_recv.at[d, i],
            {"tok": (tok + 2 * hop) % n_tok},
        )

    def side_copy(d, i):
        return remote(
            window.at[d, span(mine, i)],
            window.at[d, span(mine, i)],
            side_send.at[d, i],
            side_recv.at[d, i],
            {"tok": sibling},
        )

    def side_arrival(d, i):
        dst = window.at[d, span(theirs, i)]
        return remote(dst, dst, side_send.at[d, i], side_recv.at[d, i], {"tok": sibling})

    for hop in (3, 1):
        for i in range(PIECES):

            @pl.when(chip + hop < chips)
            def _():
                up_copy(hop, hop, i).start()

    for i in range(PIECES):
        side_copy(0, i).start()

    def own_copy(k):
        to = (place + k) % plane
        return remote(
            feat_own.at[(to % SEQS) % 2],
            feat_all.at[rank, x],
            own_send.at[k],
            feat_recv.at[rank, x],
            {"hs": half * plane + to},
        )

    def cross_copy(k):
        to = (place + k) % plane
        return remote(
            feat_cross.at[(to % SEQS) % 2],
            feat_all.at[other_rank, x],
            cross_send.at[k],
            feat_recv.at[other_rank, x],
            {"hs": half * plane + to},
        )

    def leg_copy(leg, p):
        source, target = ((feat_own, feat_relay), (feat_relay, feat_cross))[leg]
        return remote(
            source.at[p],
            target.at[p],
            leg_send.at[leg, p],
            leg_recv.at[leg, p],
            {"hs": leg_hs[p], "tok": opposite},
        )

    def spread(p):
        first = (p + place) % 2

        @pl.loop(0, plane // 2)
        def _(m):
            @pl.when(first + 2 * m > 0)
            def _():
                cross_copy(first + 2 * m).start()

    leg_copy(0, 0).start()

    @pl.loop(1, plane)
    def _(k):
        own_copy(k).start()

    feat_all[rank, x] = feat_own[x % 2]

    for load in loads[2:]:
        load.wait()

    for i in range(PIECES):
        side_arrival(0, i).wait_recv()

    def stats_part(d, n):
        at = pl.ds(n * pair, pair)
        key_rows = window[d, :, 0:HD]
        value_rows = window[d, :, HD : 2 * HD]
        scores = lax.dot_general(
            key_rows, qs[at], CONTRACT_LAST, preferred_element_type=jnp.float32
        )
        dweights = lax.dot_general(
            value_rows, us[at], CONTRACT_LAST, preferred_element_type=jnp.float32
        )
        key_pos = (chip - d) * pair + lax.broadcasted_iota(jnp.int32, (pair, pair), 0)
        allowed = (key_pos <= position) & (key_pos >= start)
        scores = jnp.where(allowed, scores * (scale * LOG2E), NEG_FILL)
        top_old = row_top[:, at]
        top = jnp.maximum(top_old, jnp.max(scores, axis=0, keepdims=True))
        exp_terms = jnp.exp2(scores - top)
        factor = jnp.exp2(top_old - top)
        row_top[:, at] = top
        row_total[:, at] = row_total[:, at] * factor + jnp.sum(exp_terms, axis=0, keepdims=True)
        row_weighted[:, at] = row_weighted[:, at] * factor + jnp.sum(
            exp_terms * dweights, axis=0, keepdims=True
        )
        exps[d, :, at] = exp_terms
        dws[d, :, at] = dweights
        tops[d, :, at] = top

    def stats_block(d):
        @pl.when((chip >= d) & (d <= reach))
        def _():
            for n in range(n_pairs):
                stats_part(d, n)

    def passed_on(d, hop, next_hops):
        for i in range(PIECES):

            @pl.when((chip >= d) & (d <= reach))
            def _():
                up_copy(d, hop, i).wait_recv()

            for hop_on in next_hops[:1]:

                @pl.when((chip >= d) & (d + hop_on <= reach) & (chip + hop_on < chips))
                def _():
                    up_copy(d + hop_on, hop_on, i).start()

            @pl.when((chip >= d) & (d <= reach))
            def _():
                side_copy(d, i).start()

        for hop_on in next_hops[1:]:
            for i in range(PIECES):

                @pl.when((chip >= d) & (d + hop_on <= reach) & (chip + hop_on < chips))
                def _():
                    up_copy(d + hop_on, hop_on, i).start()

    def joined(d):
        for i in range(PIECES):

            @pl.when((chip >= d) & (d <= reach))
            def _():
                side_arrival(d, i).wait_recv()

    @pl.loop(0, reach // 3 + 1)
    def _(turn):
        d = 3 * turn

        @pl.when(turn == 1)
        def _():
            leg_copy(0, 1).start()

        @pl.when(turn == 2)
        def _():
            leg_copy(0, 0).wait_recv()
            leg_copy(1, 0).start()

        stats_block(d)
        passed_on(d + 1, 1, (1,))
        passed_on(d + 3, 3, (3, 1))
        joined(d + 1)
        stats_block(d + 1)
        passed_on(d + 2, 1, ())
        joined(d + 2)
        stats_block(d + 2)
        joined(d + 3)

    leg_copy(0, 1).wait_recv()
    leg_copy(1, 1).start()

    inverse = 1.0 / row_total[...]
    row_delta = stats.at[3:4]
    row_delta[...] = row_weighted[...] * inverse
    row_total[...] = inverse

    def grads_part(d, n):
        at = pl.ds(n * pair, pair)
        factor = jnp.exp2(tops[d, :, at] - row_top[:, at]) * row_total[:, at]
        weights = exps[d, :, at] * factor
        dscores = (weights * (dws[d, :, at] - row_delta[:, at])).astype(jnp.bfloat16)
        weights = weights.astype(jnp.bfloat16)
        key_rows = window[d, :, 0:HD]
        key_grads = jnp.dot(dscores, qs[at], preferred_element_type=jnp.float32)
        dvalues = jnp.dot(weights, us[at], preferred_element_type=jnp.float32)
        if n == 0:
            terms[:, 0:HD] = key_grads
            terms[:, HD : 2 * HD] = dvalues
        else:
            terms[:, 0:HD] += key_grads
            terms[:, HD : 2 * HD] += dvalues
        dq_acc[:, at] += lax.dot_general(
            key_rows, dscores, CONTRACT_FIRST, preferred_element_type=jnp.float32
        )

    def rows_of(i):
        return pl.ds(i * piece, piece)

    def back_copy(d, i):
        return remote(
            sib_out.at[d, rows_of(i)],
            sib_in.at[d, rows_of(i)],
            back_send.at[d, i],
            back_recv.at[d, i],
            {"tok": sibling},
        )

    def down_copy(d, hop, i):
        return remote(
            run_out.at[d, rows_of(i)],
            run_in.at[d, rows_of(i)],
            down_send.at[d, i],
            down_recv.at[d, i],
            {"tok": (tok + n_tok - 2 * hop) % n_tok},
        )

    def grads_block(d):
        @pl.when((chip >= d) & (d <= reach))
        def _():
            for n in range(n_pairs):
                grads_part(d, n)
            sent = terms[pl.ds(pl.multiple_of(theirs, rows), rows)]
            sib_out[d, :, 0:HD] = (sent[:, 0:HD] * scale).astype(jnp.bfloat16)
            sib_out[d, :, HD : 2 * HD] = sent[:, HD : 2 * HD].astype(jnp.bfloat16)
            for i in range(PIECES):
                back_copy(d, i).start()
            kept = terms[pl.ds(pl.multiple_of(mine, rows), rows)]
            own_terms[d, :, 0:HD] = kept[:, 0:HD] * scale
            own_terms[d, :, HD : 2 * HD] = kept[:, HD : 2 * HD]

    def summed(d, i, children):
        back_copy(d, i).wait_recv()
        own_terms[d, rows_of(i)] += sib_in[d, rows_of(i)].astype(jnp.float32)
        for child in children:

            @pl.when((d + child <= reach) & (chip + child < chips))
            def _():
                down_copy(d + child, child, i).wait_recv()
                own_terms[d, rows_of(i)] += run_in[d + child, rows_of(i)].astype(jnp.float32)

    def sent_down(d, hop, children):
        for i in range(PIECES):

            @pl.when((chip >= d) & (d <= reach))
            def _():
                summed(d, i, children)
                run_out[d, rows_of(i)] = own_terms[d, rows_of(i)].astype(jnp.bfloat16)
                down_copy(d, hop, i).start()

    @pl.loop(0, reach // 3 + 1)
    def _(turn):
        d = 3 * (reach // 3 - turn)
        grads_block(d + 2)
        grads_block(d + 1)
        sent_down(d + 4, 1, (1,))
        sent_down(d + 2, 1, ())
        sent_down(d + 6, 3, (1, 3))
        grads_block(d)

        @pl.when(turn == 1)
        def _():
            leg_copy(1, 0).wait_recv()
            spread(0)

    for layer in range(layers):
        for head in range(heads):
            at = (layer * heads + head) * rows
            block = jnp.transpose(dq_acc[:, at : at + rows]) * scale
            query_grads[layer, :, head * HD : (head + 1) * HD] = block.astype(jnp.bfloat16)
    sent_down(1, 1, (1,))
    sent_down(3, 3, (1, 3))
    leg_copy(1, 1).wait_recv()
    spread(1)
    feat_all[other_rank, x] = feat_cross[x % 2]
    for i in range(PIECES):
        summed(0, i, (1, 3))

    for q in range(2):
        cut = own_terms[0, :, q * HD : (q + 1) * HD].astype(jnp.bfloat16)
        cache_grads[:, q * HD : (q + 1) * HD] = cut
        grads_out[q] = cut

    def grads_copy(k):
        to = (x + k) % SEQS
        return remote(
            grads_out.at[to // 2],
            grads_in.at[pl.ds(pl.multiple_of(x * rows, rows), rows)],
            grads_send.at[k],
            grads_recv.at[x],
            {"hs": hs - x + to},
        )

    def grads_arrival(k):
        came = (x + SEQS - k) % SEQS
        return remote(
            grads_out.at[0],
            grads_in.at[pl.ds(pl.multiple_of(came * rows, rows), rows)],
            grads_send.at[k],
            grads_recv.at[came],
            {"hs": hs},
        )

    for k in range(1, SEQS):
        grads_copy(k).start()
    grads_in[pl.ds(pl.multiple_of(x * rows, rows), rows)] = grads_out[x // 2]

    def feat_arrival(from_rank, k):
        came = (place + k) % plane
        came_rank = (from_rank // RANKS_Y) * RANKS_Y + came // SEQS
        dst = feat_all.at[came_rank, came % SEQS]
        return remote(
            dst, dst, own_send.at[k], feat_recv.at[came_rank, came % SEQS], {"hs": hs}
        )

    @pl.loop(1, plane)
    def _(k):
        feat_arrival(rank, k).wait_recv()

    for k in range(1, SEQS):
        grads_arrival(k).wait_recv()

    cut_rows = row_block // 2

    def product(r):
        block = jnp.zeros((2 * row_block, HD), jnp.float32)
        for s in range(SEQS):
            block += jnp.dot(
                feat_all[r, s],
                grads_in[s * rows : (s + 1) * rows],
                preferred_element_type=jnp.float32,
            )
        for j in range(2):
            u = 2 * r + j
            for c in range(2):
                first = j * row_block + c * cut_rows
                parts[c, u % GROUP, u // GROUP] = block[first : first + cut_rows]

    @pl.loop(0, RANKS_Y)
    def _(k):
        product(half * RANKS_Y + k)

    @pl.loop(1, plane)
    def _(k):
        feat_arrival(other_rank, k).wait_recv()

    @pl.loop(0, RANKS_Y)
    def _(k):
        product((1 - half) * RANKS_Y + k)

    def core_copy(v):
        return remote(
            near_out.at[1, v], core_in.at[v], core_send.at[v], core_recv.at[v], {"tok": sibling}
        )

    for k in (1, 2, 3, 0):
        v = (spot + k) % GROUP
        near_out[1, v] = parts[1 - core, v].astype(jnp.bfloat16)
        core_copy(v).start()

    def groups_of(turn):
        return pl.ds(2 * ((group // 2 + 1 + turn) % 2), 2)

    def near_copy(k, turn):
        v = (spot + k) % GROUP
        return remote(
            near_out.at[0, v, groups_of(turn)],
            near_in.at[GROUP - k, groups_of(turn)],
            near_send.at[k, turn],
            near_recv.at[GROUP - k, turn],
            {"tok": near_tok(k)},
        )

    for k in (1, 2, 3, 0):
        v = (spot + k) % GROUP
        core_copy(v).wait_recv()
        total = parts[core, v] + core_in[v].astype(jnp.float32)
        if k == 0:
            parts[core, v] = total
        else:
            near_out[0, v] = total.astype(jnp.bfloat16)
            near_copy(k, 0).start()
    for k in (1, 2, 3):
        near_copy(k, 1).start()

    def near_arrival(k, turn):
        return remote(
            near_out.at[0, spot, groups_of(turn)],
            near_in.at[k, groups_of(turn)],
            near_send.at[k, turn],
            near_recv.at[k, turn],
            {"tok": tok},
        )

    def far_copy(k):
        return remote(
            far_out.at[k],
            far_in.at[GROUP - k],
            far_send.at[k],
            far_recv.at[GROUP - k],
            {"tok": far_tok(k)},
        )

    odd = group % 2
    for turn, sent in ((0, (2, 3 - 2 * odd)), (1, (1 + 2 * odd,))):
        here = groups_of(turn)
        for k in range(1, GROUP):
            near_arrival(k, turn).wait_recv()
            parts[core, spot, here] += near_in[k, here].astype(jnp.float32)
        for k in sent:
            far_out[k] = parts[core, spot, (group + k) % GROUP].astype(jnp.bfloat16)
            far_copy(k).start()

    def far_arrival(k):
        return remote(far_out.at[k], far_in.at[k], far_send.at[k], far_recv.at[k], {"tok": tok})

    total = parts[core, spot, group]
    for k in range(1, GROUP):
        far_arrival(k).wait_recv()
        total = total + far_in[k].astype(jnp.float32)
    last_out[...] = total

    parity = x % 2
    owner = tok - core + parity
    same_core = core == parity

    def last_copy(to_hs, k):
        return remote(
            last_out, last_in.at[core], last_send.at[k], last_recv.at[core],
            {"hs": to_hs, "tok": owner},
        )

    last_copy(beside, 1).start()

    @pl.when(same_core)
    def _():
        last_in[core] = total

    @pl.when(jnp.logical_not(same_core))
    def _():
        last_copy(hs, 0).start()

    def last_arrival(c):
        return remote(
            last_out, last_in.at[c], last_send.at[0], last_recv.at[c], {"hs": hs, "tok": tok}
        )

    for c in range(2):

        @pl.when(jnp.logical_not(same_core & (core == c)))
        def _():
            last_arrival(c).wait_recv()

        block = last_in[c]
        width = weight_grads.shape[1]
        weight_grads[c * cut_rows : (c + 1) * cut_rows] = jnp.where(
            parity == 0, block[:, 0:width], block[:, width : 2 * width]
        )

    last_copy(beside, 1).wait_send()

    @pl.when(jnp.logical_not(same_core))
    def _():
        last_copy(hs, 0).wait_send()

    for k in range(1, GROUP):
        far_copy(k).wait_send()
        near_copy(k, 0).wait_send()
        near_copy(k, 1).wait_send()
        grads_copy(k).wait_send()
    for v in range(GROUP):
        core_copy(v).wait_send()
    for leg in range(2):
        for p in range(2):
            leg_copy(leg, p).wait_send()

    @pl.loop(1, plane)
    def _(k):
        own_copy(k).wait_send()
        cross_copy(k).wait_send()

    @pl.loop(0, reach + 1)
    def _(d):
        for i in range(PIECES):

            @pl.when(chip >= d)
            def _():
                side_copy(d, i).wait_send()
                back_copy(d, i).wait_send()

            for last, hop in ((d % 3 != 0, 1), ((d % 3 == 0) & (d > 0), 3)):

                @pl.when((chip >= d) & last)
                def _():
                    down_copy(d, hop, i).wait_send()

                @pl.when((chip + hop >= d) & (chip + hop < chips) & last)
                def _():
                    up_copy(d, hop, i).wait_send()


def shards(queries, out_grads, kv_cache, features, doc_lens):
    layers, _, rows, columns = queries.shape
    feats = features.shape[2]
    n_tok = lax.axis_size("tok")
    slots = n_tok // 4 + 1
    n_rows = layers * columns // HD * rows
    pair = 2 * rows
    ranks = 2 * RANKS_Y
    cut = feats // 8
    vmem = pl.BlockSpec(memory_space=pltpu.VMEM)
    dma = pltpu.SemaphoreType.DMA
    sems = dma((slots, PIECES))
    block = (slots, rows, 2 * HD)
    bf16, f32 = jnp.bfloat16, jnp.float32
    query_grads, cache_grads, weight_grads = pl.pallas_call(
        functools.partial(kernel, n_tok),
        out_shape=(
            jax.ShapeDtypeStruct((layers, rows, columns), bf16),
            jax.ShapeDtypeStruct((rows, 2 * HD), bf16),
            jax.ShapeDtypeStruct((feats // 4, 2 * HD // SEQS), f32),
        ),
        in_specs=[pl.BlockSpec(memory_space=pltpu.SMEM)] + [pl.BlockSpec(memory_space=pl.ANY)] * 4,
        out_specs=(vmem, vmem, vmem),
        scratch_shapes=[
            pltpu.VMEM((n_rows, HD), bf16),
            pltpu.VMEM((n_rows, HD), bf16),
            pltpu.VMEM((slots, pair, 2 * HD), bf16),
            pltpu.VMEM((slots, pair, n_rows), f32),
            pltpu.VMEM((slots, pair, n_rows), f32),
            pltpu.VMEM((slots, 1, n_rows), f32),
            pltpu.VMEM((8, n_rows), f32),
            pltpu.VMEM((HD, n_rows), f32),
            pltpu.VMEM((pair, 2 * HD), f32),
            pltpu.VMEM(block, f32),
            pltpu.VMEM(block, bf16),
            pltpu.VMEM(block, bf16),
            pltpu.VMEM(block, bf16),
            pltpu.VMEM(block, bf16),
            pltpu.VMEM((rows, feats), bf16),
            pltpu.VMEM((2, feats // 2, rows), bf16),
            pltpu.VMEM((2, feats // 2, rows), bf16),
            pltpu.VMEM((2, feats // 2, rows), bf16),
            pltpu.VMEM((ranks, SEQS, feats // 2, rows), bf16),
            pltpu.VMEM((2, rows, HD), bf16),
            pltpu.VMEM((SEQS * rows, HD), bf16),
            pltpu.VMEM((2, GROUP, GROUP, cut, HD), f32),
            pltpu.VMEM((GROUP, GROUP, cut, HD), bf16),
            pltpu.VMEM((2, GROUP, GROUP, cut, HD), bf16),
            pltpu.VMEM((GROUP, GROUP, cut, HD), bf16),
            pltpu.VMEM((GROUP, cut, HD), bf16),
            pltpu.VMEM((GROUP, cut, HD), bf16),
            pltpu.VMEM((cut, HD), f32),
            pltpu.VMEM((2, cut, HD), f32),
        ]
        + [sems] * 8
        + [dma((16,)), dma((16,)), dma((ranks, SEQS)), dma((2, 2)), dma((2, 2))]
        + [dma((2 + 2 * layers * columns // HD,))]
        + [dma((4,))] * 4
        + [dma((4, 2))] * 2
        + [dma((4,))] * 2
        + [dma((2,))] * 2,
        compiler_params=pltpu.CompilerParams(
            collective_id=0, has_side_effects=True, vmem_limit_bytes=60 * 2**20
        ),
        name="backward",
    )(doc_lens, queries[:, 0], out_grads[:, 0], kv_cache[0], features[0])
    return (query_grads[:, None], cache_grads[None], weight_grads)


def solution(mesh):
    placed = (
        P(None, "hs", "tok", None),
        P(None, "hs", "tok", None),
        P("hs", "tok", None),
        P("hs", "tok", None),
        P(),
    )
    return jax.shard_map(
        shards,
        mesh=mesh,
        in_specs=placed,
        out_specs=(P(None, "hs", "tok", None), P("hs", "tok", None), P("tok", "hs")),
        check_vma=False,
    )
```

```python
import functools

import jax
import jax.numpy as jnp
from jax import lax
from jax.experimental import pallas as pl
from jax.experimental.pallas import tpu as pltpu
from jax.sharding import PartitionSpec as P

HD = 128
SEQS = 4
RANKS_Y = 4
GROUP = 4
NEG_FILL = -1e30
PIECES = 2
LOG2E = 1.4426950408889634
MESH = pl.DeviceIdType.MESH
CONTRACT_LAST = (((1,), (1,)), ((), ()))
CONTRACT_FIRST = (((0,), (0,)), ((), ()))


def remote(src, dst, send_sem, recv_sem, device):
    return pltpu.make_async_remote_copy(
        src_ref=src,
        dst_ref=dst,
        send_sem=send_sem,
        recv_sem=recv_sem,
        device_id=device,
        device_id_type=MESH,
    )


def kernel(
    n_tok,
    doc_lens,
    queries,
    upstream,
    cache,
    features,
    query_grads,
    cache_grads,
    weight_grads,
    qs,
    us,
    window,
    exps,
    dws,
    tops,
    stats,
    dq_acc,
    terms,
    own_terms,
    sib_out,
    sib_in,
    run_out,
    run_in,
    feat_in,
    feat_own,
    feat_relay,
    feat_cross,
    feat_all,
    grads_out,
    grads_in,
    parts,
    core_in,
    near_out,
    near_in,
    far_out,
    far_in,
    last_out,
    last_in,
    up_send,
    up_recv,
    side_send,
    side_recv,
    back_send,
    back_recv,
    down_send,
    down_recv,
    own_send,
    cross_send,
    feat_recv,
    leg_send,
    leg_recv,
    load_sems,
    grads_send,
    grads_recv,
    core_send,
    core_recv,
    near_send,
    near_recv,
    far_send,
    far_recv,
    last_send,
    last_recv,
):
    layers, rows, columns = queries.shape
    heads = columns // HD
    n_rows = layers * heads * rows
    chips = n_tok // 2
    reach = n_tok // 4
    piece = rows // PIECES
    pair = 2 * rows
    n_pairs = n_rows // pair
    scale = HD ** (-0.5)

    tok = lax.axis_index("tok")
    hs = lax.axis_index("hs")
    chip = tok // 2
    core = tok % 2
    sibling = tok + 1 - 2 * core
    mine = core * rows
    theirs = (1 - core) * rows
    x = hs % SEQS
    y = (hs // SEQS) % RANKS_Y
    plane = SEQS * RANKS_Y
    half = hs // plane
    place = hs % plane
    rank = half * RANKS_Y + y
    upper = chip // (chips // 2)
    opposite = (tok + n_tok // 2) % n_tok
    kept_half = half * plane + place
    other_half = (1 - half) * plane + place
    leg_hs = (
        kept_half * upper + other_half * (1 - upper),
        kept_half * (1 - upper) + other_half * upper,
    )
    other_rank = (1 - half) * RANKS_Y + y
    beside = hs + 1 - 2 * (x % 2)
    spot = chip % GROUP
    group = chip // GROUP

    def near_tok(k):
        return (group * GROUP + (spot + k) % GROUP) * 2 + core

    def far_tok(k):
        return (((group + k) % GROUP) * GROUP + spot) * 2 + core

    def plane_hs(k):
        return half * plane + (place + k) % plane

    barrier = pltpu.get_barrier_semaphore()
    met = [{"tok": far_tok(k)} for k in range(1, GROUP)]
    met += [{"hs": leg_hs[0], "tok": opposite}, {"hs": leg_hs[1], "tok": opposite}]
    met += [{"tok": sibling}]
    met += [{"tok": near_tok(k)} for k in range(1, GROUP)]
    met += [{"hs": plane_hs(k)} for k in range(1, plane)]
    met += [{"hs": beside, "tok": sibling}]
    expected = len(met)
    for k in (1, 3):

        @pl.when(chip + k < chips)
        def _():
            pl.semaphore_signal(
                barrier, inc=1, device_id={"tok": (tok + 2 * k) % n_tok}, device_id_type=MESH
            )

        @pl.when(chip >= k)
        def _():
            pl.semaphore_signal(
                barrier,
                inc=1,
                device_id={"tok": (tok + n_tok - 2 * k) % n_tok},
                device_id_type=MESH,
            )

        expected = expected + (2 * chips - 1 - k - chip) // chips + (chip + chips - k) // chips
    for device in met:
        pl.semaphore_signal(barrier, inc=1, device_id=device, device_id_type=MESH)

    loads = [
        pltpu.make_async_copy(
            cache, window.at[0, pl.ds(pl.multiple_of(mine, rows), rows)], load_sems.at[0]
        ),
        pltpu.make_async_copy(features, feat_in, load_sems.at[1]),
    ]
    for layer in range(layers):
        for head in range(heads):
            at = (layer * heads + head) * rows
            for source, target in ((queries, qs), (upstream, us)):
                loads.append(
                    pltpu.make_async_copy(
                        source.at[layer, :, head * HD : (head + 1) * HD],
                        target.at[at : at + rows],
                        load_sems.at[len(loads)],
                    )
                )
    for load in loads:
        load.start()
    loads[1].wait()

    row_block = feat_in.shape[1] // 4
    for n in range(feat_in.shape[1] // HD):
        turned = jnp.transpose(feat_in[:, n * HD : (n + 1) * HD].astype(jnp.float32)).astype(
            jnp.bfloat16
        )
        first = n * HD
        while first < (n + 1) * HD:
            block = first // row_block
            last = min((block + 1) * row_block, (n + 1) * HD)
            to = (block // 2) * row_block + first - block * row_block
            feat_own[block % 2, to : to + last - first] = turned[
                first - n * HD : last - n * HD
            ]
            first = last

    row_top = stats.at[0:1]
    row_total = stats.at[1:2]
    row_weighted = stats.at[2:3]
    row_top[...] = jnp.full((1, n_rows), NEG_FILL, jnp.float32)
    row_total[...] = jnp.zeros((1, n_rows), jnp.float32)
    row_weighted[...] = jnp.zeros((1, n_rows), jnp.float32)
    dq_acc[...] = jnp.zeros_like(dq_acc)

    seq = x
    position = tok * rows + lax.rem(lax.broadcasted_iota(jnp.int32, (1, pair), 1), rows)
    start = jnp.zeros((1, pair), jnp.int32)
    end = jnp.int32(0)
    for k in range(doc_lens.shape[1] - 1):
        end = end + doc_lens[seq, k]
        start = jnp.where(position >= end, end, start)

    loads[0].wait()
    pl.semaphore_wait(barrier, expected)

    def span(first, i):
        return pl.ds(pl.multiple_of(first + i * piece, piece), piece)

    def up_copy(d, hop, i):
        return remote(
            window.at[d - hop, span(mine, i)],
            window.at[d, span(mine, i)],
            up_send.at[d, i],
            up_recv.at[d, i],
            {"tok": (tok + 2 * hop) % n_tok},
        )

    def side_copy(d, i):
        return remote(
            window.at[d, span(mine, i)],
            window.at[d, span(mine, i)],
            side_send.at[d, i],
            side_recv.at[d, i],
            {"tok": sibling},
        )

    def side_arrival(d, i):
        dst = window.at[d, span(theirs, i)]
        return remote(dst, dst, side_send.at[d, i], side_recv.at[d, i], {"tok": sibling})

    for hop in (3, 1):
        for i in range(PIECES):

            @pl.when(chip + hop < chips)
            def _():
                up_copy(hop, hop, i).start()

    for i in range(PIECES):
        side_copy(0, i).start()

    def own_copy(k):
        to = (place + k) % plane
        return remote(
            feat_own.at[(to % SEQS) % 2],
            feat_all.at[rank, x],
            own_send.at[k],
            feat_recv.at[rank, x],
            {"hs": half * plane + to},
        )

    def cross_copy(k):
        to = (place + k) % plane
        return remote(
            feat_cross.at[(to % SEQS) % 2],
            feat_all.at[other_rank, x],
            cross_send.at[k],
            feat_recv.at[other_rank, x],
            {"hs": half * plane + to},
        )

    def leg_copy(leg, p):
        source, target = ((feat_own, feat_relay), (feat_relay, feat_cross))[leg]
        return remote(
            source.at[p],
            target.at[p],
            leg_send.at[leg, p],
            leg_recv.at[leg, p],
            {"hs": leg_hs[p], "tok": opposite},
        )

    def spread(p):
        first = (p + place) % 2

        @pl.loop(0, plane // 2)
        def _(m):
            @pl.when(first + 2 * m > 0)
            def _():
                cross_copy(first + 2 * m).start()

    leg_copy(0, 0).start()

    @pl.loop(1, plane)
    def _(k):
        own_copy(k).start()

    feat_all[rank, x] = feat_own[x % 2]

    for load in loads[2:]:
        load.wait()

    for i in range(PIECES):
        side_arrival(0, i).wait_recv()

    def stats_part(d, n):
        at = pl.ds(n * pair, pair)
        key_rows = window[d, :, 0:HD]
        value_rows = window[d, :, HD : 2 * HD]
        scores = lax.dot_general(
            key_rows, qs[at], CONTRACT_LAST, preferred_element_type=jnp.float32
        )
        dweights = lax.dot_general(
            value_rows, us[at], CONTRACT_LAST, preferred_element_type=jnp.float32
        )
        key_pos = (chip - d) * pair + lax.broadcasted_iota(jnp.int32, (pair, pair), 0)
        allowed = (key_pos <= position) & (key_pos >= start)
        scores = jnp.where(allowed, scores * (scale * LOG2E), NEG_FILL)
        top_old = row_top[:, at]
        top = jnp.maximum(top_old, jnp.max(scores, axis=0, keepdims=True))
        exp_terms = jnp.exp2(scores - top)
        factor = jnp.exp2(top_old - top)
        row_top[:, at] = top
        row_total[:, at] = row_total[:, at] * factor + jnp.sum(exp_terms, axis=0, keepdims=True)
        row_weighted[:, at] = row_weighted[:, at] * factor + jnp.sum(
            exp_terms * dweights, axis=0, keepdims=True
        )
        exps[d, :, at] = exp_terms
        dws[d, :, at] = dweights
        tops[d, :, at] = top

    def stats_block(d):
        @pl.when((chip >= d) & (d <= reach))
        def _():
            for n in range(n_pairs):
                stats_part(d, n)

    def passed_on(d, hop, next_hops):
        for i in range(PIECES):

            @pl.when((chip >= d) & (d <= reach))
            def _():
                up_copy(d, hop, i).wait_recv()

            for hop_on in next_hops[:1]:

                @pl.when((chip >= d) & (d + hop_on <= reach) & (chip + hop_on < chips))
                def _():
                    up_copy(d + hop_on, hop_on, i).start()

            @pl.when((chip >= d) & (d <= reach))
            def _():
                side_copy(d, i).start()

        for hop_on in next_hops[1:]:
            for i in range(PIECES):

                @pl.when((chip >= d) & (d + hop_on <= reach) & (chip + hop_on < chips))
                def _():
                    up_copy(d + hop_on, hop_on, i).start()

    def joined(d):
        for i in range(PIECES):

            @pl.when((chip >= d) & (d <= reach))
            def _():
                side_arrival(d, i).wait_recv()

    @pl.loop(0, reach // 3 + 1)
    def _(turn):
        d = 3 * turn

        @pl.when(turn == 1)
        def _():
            leg_copy(0, 1).start()

        @pl.when(turn == 2)
        def _():
            leg_copy(0, 0).wait_recv()
            leg_copy(1, 0).start()

        stats_block(d)
        passed_on(d + 1, 1, (1,))
        passed_on(d + 3, 3, (3, 1))
        joined(d + 1)
        stats_block(d + 1)
        passed_on(d + 2, 1, ())
        joined(d + 2)
        stats_block(d + 2)
        joined(d + 3)

    inverse = 1.0 / row_total[...]
    row_delta = stats.at[3:4]
    row_delta[...] = row_weighted[...] * inverse
    row_total[...] = inverse

    def grads_part(d, n):
        at = pl.ds(n * pair, pair)
        factor = jnp.exp2(tops[d, :, at] - row_top[:, at]) * row_total[:, at]
        weights = exps[d, :, at] * factor
        dscores = (weights * (dws[d, :, at] - row_delta[:, at])).astype(jnp.bfloat16)
        weights = weights.astype(jnp.bfloat16)
        key_rows = window[d, :, 0:HD]
        key_grads = jnp.dot(dscores, qs[at], preferred_element_type=jnp.float32)
        dvalues = jnp.dot(weights, us[at], preferred_element_type=jnp.float32)
        if n == 0:
            terms[:, 0:HD] = key_grads
            terms[:, HD : 2 * HD] = dvalues
        else:
            terms[:, 0:HD] += key_grads
            terms[:, HD : 2 * HD] += dvalues
        dq_acc[:, at] += lax.dot_general(
            key_rows, dscores, CONTRACT_FIRST, preferred_element_type=jnp.float32
        )

    def rows_of(i):
        return pl.ds(i * piece, piece)

    def back_copy(d, i):
        return remote(
            sib_out.at[d, rows_of(i)],
            sib_in.at[d, rows_of(i)],
            back_send.at[d, i],
            back_recv.at[d, i],
            {"tok": sibling},
        )

    def down_copy(d, hop, i):
        return remote(
            run_out.at[d, rows_of(i)],
            run_in.at[d, rows_of(i)],
            down_send.at[d, i],
            down_recv.at[d, i],
            {"tok": (tok + n_tok - 2 * hop) % n_tok},
        )

    def grads_block(d):
        @pl.when((chip >= d) & (d <= reach))
        def _():
            for n in range(n_pairs):
                grads_part(d, n)
            sent = terms[pl.ds(pl.multiple_of(theirs, rows), rows)]
            sib_out[d, :, 0:HD] = (sent[:, 0:HD] * scale).astype(jnp.bfloat16)
            sib_out[d, :, HD : 2 * HD] = sent[:, HD : 2 * HD].astype(jnp.bfloat16)
            for i in range(PIECES):
                back_copy(d, i).start()
            kept = terms[pl.ds(pl.multiple_of(mine, rows), rows)]
            own_terms[d, :, 0:HD] = kept[:, 0:HD] * scale
            own_terms[d, :, HD : 2 * HD] = kept[:, HD : 2 * HD]

    def summed(d, i, children):
        back_copy(d, i).wait_recv()
        own_terms[d, rows_of(i)] += sib_in[d, rows_of(i)].astype(jnp.float32)
        for child in children:

            @pl.when((d + child <= reach) & (chip + child < chips))
            def _():
                down_copy(d + child, child, i).wait_recv()
                own_terms[d, rows_of(i)] += run_in[d + child, rows_of(i)].astype(jnp.float32)

    def sent_down(d, hop, children):
        for i in range(PIECES):

            @pl.when((chip >= d) & (d <= reach))
            def _():
                summed(d, i, children)
                run_out[d, rows_of(i)] = own_terms[d, rows_of(i)].astype(jnp.bfloat16)
                down_copy(d, hop, i).start()

    @pl.loop(0, reach // 3 + 1)
    def _(turn):
        d = 3 * (reach // 3 - turn)
        grads_block(d + 2)
        grads_block(d + 1)

        @pl.when(turn == 0)
        def _():
            leg_copy(0, 1).wait_recv()
            leg_copy(1, 1).start()

        sent_down(d + 6, 3, (1, 3))
        sent_down(d + 4, 1, (1,))
        sent_down(d + 2, 1, ())
        grads_block(d)

        @pl.when(turn == 1)
        def _():
            leg_copy(1, 0).wait_recv()
            spread(0)

    for layer in range(layers):
        for head in range(heads):
            at = (layer * heads + head) * rows
            block = jnp.transpose(dq_acc[:, at : at + rows]) * scale
            query_grads[layer, :, head * HD : (head + 1) * HD] = block.astype(jnp.bfloat16)
    sent_down(1, 1, (1,))
    sent_down(3, 3, (1, 3))
    for i in range(PIECES):
        summed(0, i, (1, 3))

    for q in range(2):
        cut = own_terms[0, :, q * HD : (q + 1) * HD].astype(jnp.bfloat16)
        cache_grads[:, q * HD : (q + 1) * HD] = cut
        grads_out[q] = cut

    def grads_copy(k):
        to = (x + k) % SEQS
        return remote(
            grads_out.at[to // 2],
            grads_in.at[pl.ds(pl.multiple_of(x * rows, rows), rows)],
            grads_send.at[k],
            grads_recv.at[x],
            {"hs": hs - x + to},
        )

    def grads_arrival(k):
        came = (x + SEQS - k) % SEQS
        return remote(
            grads_out.at[0],
            grads_in.at[pl.ds(pl.multiple_of(came * rows, rows), rows)],
            grads_send.at[k],
            grads_recv.at[came],
            {"hs": hs},
        )

    for k in range(1, SEQS):
        grads_copy(k).start()
    grads_in[pl.ds(pl.multiple_of(x * rows, rows), rows)] = grads_out[x // 2]
    leg_copy(1, 1).wait_recv()
    spread(1)
    feat_all[other_rank, x] = feat_cross[x % 2]

    def feat_arrival(from_rank, k):
        came = (place + k) % plane
        came_rank = (from_rank // RANKS_Y) * RANKS_Y + came // SEQS
        dst = feat_all.at[came_rank, came % SEQS]
        return remote(
            dst, dst, own_send.at[k], feat_recv.at[came_rank, came % SEQS], {"hs": hs}
        )

    @pl.loop(1, plane)
    def _(k):
        feat_arrival(rank, k).wait_recv()

    for k in range(1, SEQS):
        grads_arrival(k).wait_recv()

    cut_rows = row_block // 2

    def product(r):
        block = jnp.zeros((2 * row_block, HD), jnp.float32)
        for s in range(SEQS):
            block += jnp.dot(
                feat_all[r, s],
                grads_in[s * rows : (s + 1) * rows],
                preferred_element_type=jnp.float32,
            )
        for j in range(2):
            u = 2 * r + j
            for c in range(2):
                first = j * row_block + c * cut_rows
                parts[c, u % GROUP, u // GROUP] = block[first : first + cut_rows]

    @pl.loop(0, RANKS_Y)
    def _(k):
        product(half * RANKS_Y + k)

    @pl.loop(1, plane)
    def _(k):
        feat_arrival(other_rank, k).wait_recv()

    @pl.loop(0, RANKS_Y)
    def _(k):
        product((1 - half) * RANKS_Y + k)

    def core_copy(v):
        return remote(
            near_out.at[1, v], core_in.at[v], core_send.at[v], core_recv.at[v], {"tok": sibling}
        )

    for k in (1, 2, 3, 0):
        v = (spot + k) % GROUP
        near_out[1, v] = parts[1 - core, v].astype(jnp.bfloat16)
        core_copy(v).start()

    def groups_of(turn):
        return pl.ds(2 * ((group // 2 + 1 + turn) % 2), 2)

    def near_copy(k, turn):
        v = (spot + k) % GROUP
        return remote(
            near_out.at[0, v, groups_of(turn)],
            near_in.at[GROUP - k, groups_of(turn)],
            near_send.at[k, turn],
            near_recv.at[GROUP - k, turn],
            {"tok": near_tok(k)},
        )

    for k in (1, 2, 3, 0):
        v = (spot + k) % GROUP
        core_copy(v).wait_recv()
        total = parts[core, v] + core_in[v].astype(jnp.float32)
        if k == 0:
            parts[core, v] = total
        else:
            near_out[0, v] = total.astype(jnp.bfloat16)
            near_copy(k, 0).start()
    for k in (1, 2, 3):
        near_copy(k, 1).start()

    def near_arrival(k, turn):
        return remote(
            near_out.at[0, spot, groups_of(turn)],
            near_in.at[k, groups_of(turn)],
            near_send.at[k, turn],
            near_recv.at[k, turn],
            {"tok": tok},
        )

    def far_copy(k):
        return remote(
            far_out.at[k],
            far_in.at[GROUP - k],
            far_send.at[k],
            far_recv.at[GROUP - k],
            {"tok": far_tok(k)},
        )

    odd = group % 2
    for turn, sent in ((0, (2, 3 - 2 * odd)), (1, (1 + 2 * odd,))):
        here = groups_of(turn)
        for k in range(1, GROUP):
            near_arrival(k, turn).wait_recv()
            parts[core, spot, here] += near_in[k, here].astype(jnp.float32)
        for k in sent:
            far_out[k] = parts[core, spot, (group + k) % GROUP].astype(jnp.bfloat16)
            far_copy(k).start()

    def far_arrival(k):
        return remote(far_out.at[k], far_in.at[k], far_send.at[k], far_recv.at[k], {"tok": tok})

    total = parts[core, spot, group]
    for k in range(1, GROUP):
        far_arrival(k).wait_recv()
        total = total + far_in[k].astype(jnp.float32)
    last_out[...] = total

    parity = x % 2
    owner = tok - core + parity
    same_core = core == parity

    def last_copy(to_hs, k):
        return remote(
            last_out, last_in.at[core], last_send.at[k], last_recv.at[core],
            {"hs": to_hs, "tok": owner},
        )

    last_copy(beside, 1).start()

    @pl.when(same_core)
    def _():
        last_in[core] = total

    @pl.when(jnp.logical_not(same_core))
    def _():
        last_copy(hs, 0).start()

    def last_arrival(c):
        return remote(
            last_out, last_in.at[c], last_send.at[0], last_recv.at[c], {"hs": hs, "tok": tok}
        )

    for c in range(2):

        @pl.when(jnp.logical_not(same_core & (core == c)))
        def _():
            last_arrival(c).wait_recv()

        block = last_in[c]
        width = weight_grads.shape[1]
        weight_grads[c * cut_rows : (c + 1) * cut_rows] = jnp.where(
            parity == 0, block[:, 0:width], block[:, width : 2 * width]
        )

    last_copy(beside, 1).wait_send()

    @pl.when(jnp.logical_not(same_core))
    def _():
        last_copy(hs, 0).wait_send()

    for k in range(1, GROUP):
        far_copy(k).wait_send()
        near_copy(k, 0).wait_send()
        near_copy(k, 1).wait_send()
        grads_copy(k).wait_send()
    for v in range(GROUP):
        core_copy(v).wait_send()
    for leg in range(2):
        for p in range(2):
            leg_copy(leg, p).wait_send()

    @pl.loop(1, plane)
    def _(k):
        own_copy(k).wait_send()
        cross_copy(k).wait_send()

    @pl.loop(0, reach + 1)
    def _(d):
        for i in range(PIECES):

            @pl.when(chip >= d)
            def _():
                side_copy(d, i).wait_send()
                back_copy(d, i).wait_send()

            for last, hop in ((d % 3 != 0, 1), ((d % 3 == 0) & (d > 0), 3)):

                @pl.when((chip >= d) & last)
                def _():
                    down_copy(d, hop, i).wait_send()

                @pl.when((chip + hop >= d) & (chip + hop < chips) & last)
                def _():
                    up_copy(d, hop, i).wait_send()


def shards(queries, out_grads, kv_cache, features, doc_lens):
    layers, _, rows, columns = queries.shape
    feats = features.shape[2]
    n_tok = lax.axis_size("tok")
    slots = n_tok // 4 + 1
    n_rows = layers * columns // HD * rows
    pair = 2 * rows
    ranks = 2 * RANKS_Y
    cut = feats // 8
    vmem = pl.BlockSpec(memory_space=pltpu.VMEM)
    dma = pltpu.SemaphoreType.DMA
    sems = dma((slots, PIECES))
    block = (slots, rows, 2 * HD)
    bf16, f32 = jnp.bfloat16, jnp.float32
    query_grads, cache_grads, weight_grads = pl.pallas_call(
        functools.partial(kernel, n_tok),
        out_shape=(
            jax.ShapeDtypeStruct((layers, rows, columns), bf16),
            jax.ShapeDtypeStruct((rows, 2 * HD), bf16),
            jax.ShapeDtypeStruct((feats // 4, 2 * HD // SEQS), f32),
        ),
        in_specs=[pl.BlockSpec(memory_space=pltpu.SMEM)] + [pl.BlockSpec(memory_space=pl.ANY)] * 4,
        out_specs=(vmem, vmem, vmem),
        scratch_shapes=[
            pltpu.VMEM((n_rows, HD), bf16),
            pltpu.VMEM((n_rows, HD), bf16),
            pltpu.VMEM((slots, pair, 2 * HD), bf16),
            pltpu.VMEM((slots, pair, n_rows), f32),
            pltpu.VMEM((slots, pair, n_rows), f32),
            pltpu.VMEM((slots, 1, n_rows), f32),
            pltpu.VMEM((8, n_rows), f32),
            pltpu.VMEM((HD, n_rows), f32),
            pltpu.VMEM((pair, 2 * HD), f32),
            pltpu.VMEM(block, f32),
            pltpu.VMEM(block, bf16),
            pltpu.VMEM(block, bf16),
            pltpu.VMEM(block, bf16),
            pltpu.VMEM(block, bf16),
            pltpu.VMEM((rows, feats), bf16),
            pltpu.VMEM((2, feats // 2, rows), bf16),
            pltpu.VMEM((2, feats // 2, rows), bf16),
            pltpu.VMEM((2, feats // 2, rows), bf16),
            pltpu.VMEM((ranks, SEQS, feats // 2, rows), bf16),
            pltpu.VMEM((2, rows, HD), bf16),
            pltpu.VMEM((SEQS * rows, HD), bf16),
            pltpu.VMEM((2, GROUP, GROUP, cut, HD), f32),
            pltpu.VMEM((GROUP, GROUP, cut, HD), bf16),
            pltpu.VMEM((2, GROUP, GROUP, cut, HD), bf16),
            pltpu.VMEM((GROUP, GROUP, cut, HD), bf16),
            pltpu.VMEM((GROUP, cut, HD), bf16),
            pltpu.VMEM((GROUP, cut, HD), bf16),
            pltpu.VMEM((cut, HD), f32),
            pltpu.VMEM((2, cut, HD), f32),
        ]
        + [sems] * 8
        + [dma((16,)), dma((16,)), dma((ranks, SEQS)), dma((2, 2)), dma((2, 2))]
        + [dma((2 + 2 * layers * columns // HD,))]
        + [dma((4,))] * 4
        + [dma((4, 2))] * 2
        + [dma((4,))] * 2
        + [dma((2,))] * 2,
        compiler_params=pltpu.CompilerParams(
            collective_id=0, has_side_effects=True, vmem_limit_bytes=60 * 2**20
        ),
        name="backward",
    )(doc_lens, queries[:, 0], out_grads[:, 0], kv_cache[0], features[0])
    return (query_grads[:, None], cache_grads[None], weight_grads)


def solution(mesh):
    placed = (
        P(None, "hs", "tok", None),
        P(None, "hs", "tok", None),
        P("hs", "tok", None),
        P("hs", "tok", None),
        P(),
    )
    return jax.shard_map(
        shards,
        mesh=mesh,
        in_specs=placed,
        out_specs=(P(None, "hs", "tok", None), P("hs", "tok", None), P("tok", "hs")),
        check_vma=False,
    )
```
